256 devices in a mesh: rows: 16 (over z_lo, x, core), cols: 16 (over z_hi, y).
Axes of the slice: x: 4, y: 4, z: 8 (z_hi: 4, z_lo: 2; z = z_hi * 2 + z_lo), core: 2. Of those that a mesh axis runs over, the one named last changes fastest.
Arguments:
- search_vectors: bfloat16 [16384, 1024], P(('rows', 'cols')), may hold values from -6 to 6
- tile_values: bfloat16 [256, 64, 512], P('rows'), may hold values from -0.25 to 0.25
- block_columns: int32 [256, 8], P('rows'), may hold values from -4 to 259, as said below
Outputs:
- filtered: bfloat16 [16384, 1024], P(('rows', 'cols'))
- gram: float32 [1024, 1024], P('cols')
The draws below stay inside these ranges and needn't reach their ends.
Inputs may be any that keep to these rules, and one draw needn't show every extreme that they name: `block_columns`: row b names 8 distinct block columns, each within 4 of b, always including b - 4, b and b + 4; block columns outside 0 to 255 stand for zero tiles.
All inputs are finite; a program needn't handle non-finite values.
Results may differ from the reference program's by a relative error of at most 0.023.
Values may be sent and summed in bfloat16 or wider, within the bound.
A program may use at most 64 MiB of HBM per device.

```python
import jax
import jax.numpy as jnp
from jax import lax

M = 1024
TILE = 64
KT = 8
HALO = 4
DEGREE = 8
BLK_DEV = 16
NBLK = 256
NROWS = 16384
N_ROWS = 16


def draw_block_columns(key, part):
    subkeys = jax.random.split(key, NBLK)
    inner = jnp.concatenate([jnp.arange(1 - HALO, 0), jnp.arange(1, HALO)]).astype(jnp.int32)

    def choose(subkey):
        return jax.random.permutation(subkey, inner)[:KT - 3]
    chosen = jax.vmap(choose)(subkeys)
    anchors = jnp.arange(NBLK, dtype=jnp.int32)[:, None]
    outer_offsets = jnp.broadcast_to(jnp.array([-HALO, 0, HALO], jnp.int32), (NBLK, 3))
    offsets = jnp.concatenate([outer_offsets, chosen], axis=1)
    return (anchors + offsets).astype(jnp.int32)


def levels(own_key, extent, cuts, least, high):
    gain = 1.0
    for axis_at, shards_of in cuts:
        steps = jax.random.uniform(jax.random.fold_in(jax.random.fold_in(own_key, 6), axis_at), (shards_of,), jnp.float32, least / len(cuts), high / len(cuts))
        gain = gain * jnp.repeat(jnp.exp(steps), extent[axis_at] // shards_of).reshape((-1,) + (1,) * (len(extent) - 1 - axis_at))
    return gain


def noise(stream_key, extent, scale, bound, pieces=(), kind=jnp.bfloat16):
    level = levels(stream_key, extent, pieces, -0.22, 0.18) if pieces else 1.0
    result = jax.random.normal(stream_key, extent, jnp.float32) * scale * level
    return jnp.minimum(jnp.maximum(result, -bound), bound).astype(kind)


def setup_inputs(seed: int = 0) -> dict:
    arg_keys = jax.random.split(jax.random.key(seed), 4)
    return {
        "search_vectors": noise(arg_keys[0], (NROWS, M), 1.0, 6.0, ((0, 256),)),
        "tile_values": noise(arg_keys[1], (NBLK, TILE, KT * TILE), (KT * TILE) ** -0.5, 0.25, ((0, 16),)),
        "block_columns": draw_block_columns(jax.random.fold_in(arg_keys[3], 71), 0),
    }


shift_value = 0.1
half_width = 2.0


def reference(search_vectors, tile_values, block_columns):
    grouped_tiles = tile_values.reshape(N_ROWS, BLK_DEV, TILE, KT * TILE)
    grouped_index = block_columns.reshape(N_ROWS, BLK_DEV, KT)

    def filter_step(iterate):
        rounded = iterate.astype(jnp.bfloat16)
        padded = jnp.pad(rounded.reshape(NBLK, TILE, M), ((HALO, HALO), (0, 0), (0, 0)))

        def one_group(operands):
            tile_group, index_group = operands
            picked = padded[(index_group + HALO).astype(jnp.int32)]
            picked = picked.reshape(BLK_DEV, KT * TILE, M)
            return jnp.einsum("bij,bjc->bic", tile_group.astype(jnp.float32), picked.astype(jnp.float32))

        mapped = lax.map(one_group, (grouped_tiles, grouped_index))
        product = mapped.reshape(NROWS, M)
        return (product - shift_value * iterate) / half_width

    previous = search_vectors.astype(jnp.float32)
    current = filter_step(previous)
    for degree_step in range(DEGREE - 1):
        following = 2.0 * filter_step(current) - previous
        previous, current = current, following
    filtered = current.astype(jnp.bfloat16)
    gram = lax.dot_general(filtered, filtered, (((0,), (0,)), ((), ())), preferred_element_type=jnp.float32)
    return filtered, gram * (1.0 / NROWS)
```

```python
import functools

import jax
import jax.numpy as jnp
from jax import lax
from jax.experimental import pallas as pl
from jax.experimental.pallas import tpu as pltpu
from jax.sharding import PartitionSpec as P

MESH = pl.DeviceIdType.MESH
BF, F32 = jnp.bfloat16, jnp.float32

TILE = 64
OWN = 16
SIDE = 12
GROUP = 256
WIN = 768
SCALE = 1.0 / 16384

A2A, TIL, IDX, VEC, CUR, OLD = 0, 16, 18, 20, 22, 24
QUART, GATH, PAIR, XRED, ZRED, SPREAD, COUNT = 26, 30, 34, 38, 42, 50, 66


def swap(v):
    return jnp.concatenate([v[:, 64:], v[:, :64]], axis=1)


def pack(block):
    return jnp.concatenate([block[:32], block[32:]], axis=1)


def kernel(
    x_ref, cols_ref, tiles_ref, out_ref, gram_ref,
    xs, xr, tv, th, ab, abh, band, hx, hp, w, y, fp, op, c1, fy, gs, gr, gf, xsnd, xrcv, zs, zr, ro,
    local_sem, ss, rs,
):
    r, c = lax.axis_index("rows"), lax.axis_index("cols")
    yy, zh = lax.rem(c, 4), c // 4
    core, x, zl = lax.rem(r, 2), lax.rem(r // 2, 4), r // 8
    z = zh * 2 + zl

    def remote(src, dst, number, device):
        return pltpu.make_async_remote_copy(
            src_ref=src, dst_ref=dst, send_sem=ss.at[number], recv_sem=rs.at[number],
            device_id=device, device_id_type=MESH,
        )

    own_tiles = pltpu.make_async_copy(tiles_ref, tv, local_sem)
    own_tiles.start()

    barrier = pltpu.get_barrier_semaphore()

    def greet(device):
        pl.semaphore_signal(barrier, inc=1, device_id=device, device_id_type=MESH)

    for i in range(1, 16):
        greet((r, lax.rem(c + i, 16)))
        greet((lax.rem(r + i, 16), c))
    for i in range(1, 4):
        greet((lax.rem(r + 8, 16), lax.rem(zh + i, 4) * 4 + yy))

    for g in range(16):
        xs[g] = pack(x_ref[:, g * 64 : (g + 1) * 64])

    low = lax.broadcasted_iota(jnp.int32, (1, 128), 1) < 64
    for b in range(OWN):
        base = r * OWN + (b // 4) * 4 - 4
        for p in range(4):
            even, odd = cols_ref[b, 2 * p] - base, cols_ref[b, 2 * p + 1] - base
            ab[b, p : p + 1, :] = jnp.where(low, even, odd - 1).astype(F32)
            ab[b, 4 + p : 5 + p, :] = jnp.where(low, odd, even - 1).astype(F32)

    pl.semaphore_wait(barrier, 33)

    a2a = []
    for i in range(1, 16):
        to = lax.rem(c + i, 16)
        copy = remote(xs.at[to], xr.at[c], A2A + i, (r, to))
        copy.start()
        a2a.append(copy)
    xr[c] = xs[c]

    has_low, has_high = r > 0, r < 15
    up, down = jnp.minimum(r + 1, 15), jnp.maximum(r - 1, 0)

    def both_sides(number, to_up, to_down, low_dst, high_dst):
        a = remote(to_up, low_dst, number, (up, c))
        b = remote(to_down, high_dst, number + 1, (down, c))
        pl.when(has_high)(a.start)
        pl.when(has_low)(b.start)
        return a, b

    def arrived(pair):
        pl.when(has_low)(pair[0].wait_recv)
        pl.when(has_high)(pair[1].wait_recv)

    def sent(pair):
        pl.when(has_high)(pair[0].wait_send)
        pl.when(has_low)(pair[1].wait_send)

    idx = both_sides(IDX, ab.at[pl.ds(4, SIDE)], ab.at[pl.ds(0, SIDE)], abh.at[0], abh.at[1])
    til = both_sides(
        TIL, tiles_ref.at[pl.ds(4, SIDE)], tiles_ref.at[pl.ds(0, SIDE)], th.at[0], th.at[1]
    )

    def place(tiles, where, first, count):
        def body(b, carry):
            at = pl.multiple_of((first + b) * TILE, TILE)
            sums = [None] * 6
            for p in range(4):
                src = tiles[b, :, p * 128 : (p + 1) * 128]
                for piece, row in ((src, p), (swap(src), 4 + p)):
                    lanes = where[b, row : row + 1, :]
                    for j in range(6):
                        term = piece * jnp.where(lanes == 2.0 * j, 1.0, 0.0).astype(BF)
                        sums[j] = term if sums[j] is None else sums[j] + term
            for j in range(6):
                band[pl.ds(at, TILE), j * 128 : (j + 1) * 128] = sums[j]
            return carry

        lax.fori_loop(0, count, body, 0)

    own_tiles.wait()
    place(tv, ab, SIDE, OWN)

    def unpack_to(packed, first, targets):
        for b in range(OWN):
            v = packed[b]
            for half in range(2):
                rows = pl.ds((first + b) * TILE + half * 32, 32)
                piece = v[:, half * 64 : (half + 1) * 64]
                for ref in targets:
                    ref[rows, :] = piece.astype(ref.dtype)

    for copy in a2a:
        copy.wait_recv()
    vec = both_sides(VEC, xr, xr, hx.at[0], hx.at[1])
    unpack_to(xr, OWN, (w.at[0], y.at[0]))

    edge = lambda side: has_low if side == 0 else has_high

    def zero(ref, first, count):
        ref[pl.ds(first, count), :] = jnp.zeros((count, ref.shape[1]), ref.dtype)

    arrived(idx)
    arrived(til)
    for side in range(2):
        first = (SIDE + OWN) * side

        @pl.when(edge(side))
        def _(side=side, first=first):
            place(th.at[side], abh.at[side], first, SIDE)

        @pl.when(jnp.logical_not(edge(side)))
        def _(side=side, first=first):
            zero(band, first * TILE, SIDE * TILE)
            for k in range(2):
                zero(w.at[k], side * 2 * OWN * TILE, OWN * TILE)
                zero(y.at[k], side * 2 * OWN * TILE, OWN * TILE)

    arrived(vec)
    for side in range(2):

        @pl.when(edge(side))
        def _(side=side):
            unpack_to(hx.at[side], side * 2 * OWN, (w.at[0], y.at[0]))

    def step(number, first, count):
        now, later = number % 2, (number + 1) % 2

        def body(i, carry):
            for k in range(2):
                g = first + 2 * i + k
                rows = pl.ds(pl.multiple_of(g * GROUP, GROUP), GROUP)
                left = pl.ds(pl.multiple_of((g - 1) * GROUP, GROUP), GROUP)
                window = pl.ds(pl.multiple_of((g - 1) * GROUP, GROUP), WIN)
                product = jnp.dot(band[left, :], w[now, window, :], preferred_element_type=F32)
                if number == 0:
                    new = (product - 0.1 * y[now, rows, :]) * 0.5
                else:
                    new = product - 0.1 * y[now, rows, :] - y[later, rows, :]
                y[later, rows, :] = new
                w[later, rows, :] = new.astype(BF)
            return carry

        lax.fori_loop(0, count // 2, body, 0)

    for n in range(4):
        step(n, 1 + n, 10 - 2 * n)

    def pack_own(src, dst):
        for b in range(OWN):
            dst[b] = pack(src[pl.ds((OWN + b) * TILE, TILE), :]).astype(BF)

    pack_own(w.at[0], fp.at[0])
    cur = both_sides(CUR, fp.at[0], fp.at[0], hp.at[0], hp.at[1])
    pack_own(y.at[1], op)
    old = both_sides(OLD, op, op, hp.at[2], hp.at[3])
    arrived(cur)
    arrived(old)
    for side in range(2):

        @pl.when(edge(side))
        def _(side=side):
            unpack_to(hp.at[side], side * 2 * OWN, (w.at[0], y.at[0]))
            unpack_to(hp.at[2 + side], side * 2 * OWN, (y.at[1],))

    for n in range(4):
        step(4 + n, 1 + n, 10 - 2 * n)

    pack_own(w.at[0], fp.at[1])

    quart = []
    for i in range(1, 4):
        to = lax.rem(zh + i, 4)
        copy = remote(fp.at[1, pl.ds(to * 4, 4)], c1.at[zh], QUART + i, (r, to * 4 + yy))
        copy.start()
        quart.append(copy)
    c1[zh] = fp[1, pl.ds(zh * 4, 4)]
    for copy in quart:
        copy.wait_recv()
    for b in range(4):
        for pair in range(2):
            left, right = c1[2 * pair, b], c1[2 * pair + 1, b]
            for half in range(2):
                lanes = slice(half * 64, (half + 1) * 64)
                fy[yy, pl.ds(b * TILE + half * 32, 32), pair * 128 : (pair + 1) * 128] = (
                    jnp.concatenate([left[:, lanes], right[:, lanes]], axis=1)
                )

    gath = []
    for i in range(1, 4):
        copy = remote(fy.at[yy], fy.at[yy], GATH + i, (r, zh * 4 + lax.rem(yy + i, 4)))
        copy.start()
        gath.append(copy)
    mine_t = fy[yy].astype(F32).T.astype(BF)
    for copy in gath:
        copy.wait_recv()

    pair_dev = (r + 1 - 2 * core, c)
    pairs = []
    for k in range(4):
        gs[k] = jnp.dot(
            mine_t, fy[(1 - core) * 2 + k // 2, :, (k % 2) * 128 : (k % 2 + 1) * 128],
            preferred_element_type=F32,
        ).astype(BF)
        copy = remote(gs.at[k], gr.at[k], PAIR + k, pair_dev)
        copy.start()
        pairs.append(copy)
    for k in range(4):
        gf[k] = jnp.dot(
            mine_t, fy[core * 2 + k // 2, :, (k % 2) * 128 : (k % 2 + 1) * 128],
            preferred_element_type=F32,
        )

    rows = pl.ds(pl.multiple_of(yy * TILE, TILE), TILE)
    for h in range(4):
        for p in range(2):
            lanes = slice(h * 64, (h + 1) * 64)
            out_ref[:, h * 256 + p * 128 : h * 256 + (p + 1) * 128] = jnp.concatenate(
                [fy[2 * p, rows, lanes], fy[2 * p + 1, rows, lanes]], axis=1
            )

    for k in range(4):
        pairs[k].wait_recv()
        total = gf[k] + gr[k].astype(F32)
        gf[k] = total
        xsnd[k] = total.astype(BF)
    xred = []
    for i in range(1, 4):
        to = lax.rem(x + i, 4)
        copy = remote(xsnd.at[to], xrcv.at[i], XRED + i, (zl * 8 + to * 2 + core, c))
        copy.start()
        xred.append(copy)
    total = gf[x]
    for i in range(1, 4):
        xred[i - 1].wait_recv()
        total = total + xrcv[i].astype(F32)
    gf[x] = total
    zs[...] = total.astype(BF)

    zred = []
    for i in range(1, 8):
        to = lax.rem(z + i, 8)
        device = (lax.rem(to, 2) * 8 + x * 2 + core, (to // 2) * 4 + yy)
        copy = remote(zs.at[pl.ds(pl.multiple_of(to * 32, 32), 32)], zr.at[i], ZRED + i, device)
        copy.start()
        zred.append(copy)
    total = gf[x, pl.ds(pl.multiple_of(z * 32, 32), 32), :]
    for i in range(1, 8):
        zred[i - 1].wait_recv()
        total = total + zr[i].astype(F32)
    ro[r] = total * SCALE

    spread = []
    for i in range(1, 16):
        copy = remote(ro.at[r], ro.at[r], SPREAD + i, (lax.rem(r + i, 16), c))
        copy.start()
        spread.append(copy)

    sent(idx)
    sent(til)
    sent(vec)
    sent(cur)
    sent(old)
    for copy in a2a + quart + gath + pairs + xred + zred:
        copy.wait_send()
    for copy in spread:
        copy.wait_recv()
    for l in range(2):
        for h in range(4):
            for p in range(2):
                lanes = slice((h % 2) * 64, (h % 2 + 1) * 64)
                at = [l * 8 + (k * 2 + h // 2) * 2 + p for k in range(2)]
                gram_ref[l * 32 : (l + 1) * 32, h * 256 + p * 128 : h * 256 + (p + 1) * 128] = (
                    jnp.concatenate([ro[at[0]][:, lanes], ro[at[1]][:, lanes]], axis=1)
                )
    for copy in spread:
        copy.wait_send()


def per_device(search_vectors, tile_values, block_columns):
    ext = 3 * OWN * TILE
    return pl.pallas_call(
        kernel,
        out_shape=(
            jax.ShapeDtypeStruct((64, 1024), BF),
            jax.ShapeDtypeStruct((64, 1024), F32),
        ),
        in_specs=[
            pl.BlockSpec(memory_space=pltpu.VMEM),
            pl.BlockSpec(memory_space=pltpu.SMEM),
            pl.BlockSpec(memory_space=pl.ANY),
        ],
        out_specs=(pl.BlockSpec(memory_space=pltpu.VMEM), pl.BlockSpec(memory_space=pltpu.VMEM)),
        scratch_shapes=[
            pltpu.VMEM((16, 32, 128), BF),
            pltpu.VMEM((16, 32, 128), BF),
            pltpu.VMEM((OWN, TILE, 512), BF),
            pltpu.VMEM((2, SIDE, TILE, 512), BF),
            pltpu.VMEM((OWN, 8, 128), F32),
            pltpu.VMEM((2, SIDE, 8, 128), F32),
            pltpu.VMEM(((2 * SIDE + OWN) * TILE, WIN), BF),
            pltpu.VMEM((2, 16, 32, 128), BF),
            pltpu.VMEM((4, 16, 32, 128), BF),
            pltpu.VMEM((2, ext, 64), BF),
            pltpu.VMEM((2, ext, 64), F32),
            pltpu.VMEM((2, 16, 32, 128), BF),
            pltpu.VMEM((16, 32, 128), BF),
            pltpu.VMEM((4, 4, 32, 128), BF),
            pltpu.VMEM((4, 256, 256), BF),
            pltpu.VMEM((4, 256, 128), BF),
            pltpu.VMEM((4, 256, 128), BF),
            pltpu.VMEM((4, 256, 128), F32),
            pltpu.VMEM((4, 256, 128), BF),
            pltpu.VMEM((4, 256, 128), BF),
            pltpu.VMEM((256, 128), BF),
            pltpu.VMEM((8, 32, 128), BF),
            pltpu.VMEM((16, 32, 128), F32),
            pltpu.SemaphoreType.DMA,
            pltpu.SemaphoreType.DMA((COUNT,)),
            pltpu.SemaphoreType.DMA((COUNT,)),
        ],
        compiler_params=pltpu.CompilerParams(
            collective_id=0, has_side_effects=True, vmem_limit_bytes=48 * 1024 * 1024
        ),
        name="filter_and_gram",
    )(search_vectors, block_columns, tile_values)


def solution(mesh):
    return jax.shard_map(
        per_device,
        mesh=mesh,
        in_specs=(P(("rows", "cols"), None), P("rows", None, None), P("rows", None)),
        out_specs=(P(("rows", "cols"), None), P("cols", None)),
        check_vma=False,
    )
```

```python
import jax
import jax.numpy as jnp
from jax import lax
from jax.experimental import pallas as pl
from jax.experimental.pallas import tpu as pltpu
from jax.sharding import PartitionSpec as P

MESH = pl.DeviceIdType.MESH
BF, F32 = jnp.bfloat16, jnp.float32

TILE = 64
OWN = 16
GROUP = 256
WIN = 768
SCALE = 1.0 / 16384

A2A, TIL, IDX, VEC, EARLY, OLD, LATE = 0, 16, 22, 24, 26, 28, 30
QUART, GATH, PAIR, XRED, ZRED, SPREAD, COUNT = 32, 36, 52, 56, 60, 68, 84


def swap(v):
    return jnp.concatenate([v[:, 64:], v[:, :64]], axis=1)


def pack(block):
    return jnp.concatenate([block[:32], block[32:]], axis=1)


def kernel(
    x_hbm, cols_hbm, tiles_hbm, out_ref, gram_ref,
    x_ref, cols_ref, xs, xr, tv, th, idxv, idxh, idxs, slab, band, hx, hp, ho, w, y,
    fp, op, fq, pc, fy, gs, gr, gf, xsnd, xrcv, zs, zr, ro, local_sem, ss, rs,
):
    r, c = lax.axis_index("rows"), lax.axis_index("cols")
    yy, zh = lax.rem(c, 4), c // 4
    core, x, zl = lax.rem(r, 2), lax.rem(r // 2, 4), r // 8
    z = zh * 2 + zl

    def remote(src, dst, number, device):
        return pltpu.make_async_remote_copy(
            src_ref=src, dst_ref=dst, send_sem=ss.at[number], recv_sem=rs.at[number],
            device_id=device, device_id_type=MESH,
        )

    own_x = pltpu.make_async_copy(x_hbm, x_ref, local_sem.at[0])
    own_cols = pltpu.make_async_copy(cols_hbm, cols_ref, local_sem.at[1])
    own_tiles = pltpu.make_async_copy(tiles_hbm, tv, local_sem.at[2])

    barrier = pltpu.get_barrier_semaphore()

    def greet(device):
        pl.semaphore_signal(barrier, inc=1, device_id=device, device_id_type=MESH)

    for i in (8, 7, 9, 6, 10, 5, 11, 4, 12, 3, 13, 2, 14, 1, 15):
        greet((r, lax.rem(c + i, 16)))
        greet((lax.rem(r + i, 16), c))
    for i in range(1, 4):
        greet((lax.rem(r + 8, 16), lax.rem(zh + i, 4) * 4 + yy))
    own_x.start()
    own_cols.start()
    own_tiles.start()

    has_low, has_high = r > 0, r < 15
    edges = (has_low, has_high)
    up, down = jnp.minimum(r + 1, 15), jnp.maximum(r - 1, 0)

    def zero(ref, first, count):
        ref[pl.ds(first, count), :] = jnp.zeros((count, ref.shape[1]), ref.dtype)

    for side in range(2):

        @pl.when(jnp.logical_not(edges[side]))
        def _(side=side):
            zero(band, 7 * side * GROUP, 3 * GROUP)
            for k in range(2):
                zero(w.at[k], side * 8 * GROUP, 4 * GROUP)
                zero(y.at[k], side * 8 * GROUP, 4 * GROUP)

    for u in range(4):
        slab[u, 8] = jnp.zeros((TILE, 128), BF)

    own_x.wait()
    for g in range(16):
        xs[g] = pack(x_ref[:, g * 64 : (g + 1) * 64])

    own_cols.wait()
    slot = lax.broadcasted_iota(jnp.int32, (16, OWN), 0)
    first_col = r * OWN + (lax.broadcasted_iota(jnp.int32, (8, OWN), 1) // 4) * 4 - 4
    places = cols_ref[...] - first_col
    slabs = jnp.full((16, OWN), 8, jnp.int32)
    for k in range(8):
        which = jnp.where(lax.rem(slot, 2) == 0, k, k + 1 - 2 * (k % 2))
        slabs = jnp.where(slot == places[k : k + 1, :], which, slabs)
    idxv[...] = jnp.zeros_like(idxv)
    idxv[:, :OWN] = slabs

    pl.semaphore_wait(barrier, 33)

    a2a = []
    for i in (8, 7, 9, 6, 10, 5, 11, 4, 12, 3, 13, 2, 14, 1, 15):
        to = lax.rem(c + i, 16)
        copy = remote(xs.at[to], xr.at[c], A2A + i, (r, to))
        copy.start()
        a2a.append(copy)

    def both_sides(number, to_up, to_down, low_dst, high_dst):
        a = remote(to_up, low_dst, number, (up, c))
        b = remote(to_down, high_dst, number + 1, (down, c))
        pl.when(has_high)(a.start)
        pl.when(has_low)(b.start)
        return a, b

    def arrived(pair):
        pl.when(has_low)(pair[0].wait_recv)
        pl.when(has_high)(pair[1].wait_recv)

    def sent(pair):
        pl.when(has_high)(pair[0].wait_send)
        pl.when(has_low)(pair[1].wait_send)

    idx = both_sides(IDX, idxv, idxv, idxh.at[0], idxh.at[1])
    til = [
        both_sides(
            TIL + 2 * n, tiles_hbm.at[pl.ds(4 * (3 - n), 4)], tiles_hbm.at[pl.ds(4 * n, 4)],
            th.at[0, n], th.at[1, n],
        )
        for n in range(3)
    ]
    xr[c] = xs[c]

    low_lanes = lax.broadcasted_iota(jnp.int32, (TILE, 128), 1) < 64

    def place(tiles, source, first, at):
        for u in range(4):
            for p in range(4):
                piece = tiles[u, :, p * 128 : (p + 1) * 128]
                slab[u, 2 * p] = piece
                slab[u, 2 * p + 1] = swap(piece)
            for j in range(6):
                left = slab[u, idxs[source, 2 * j, first + u]]
                right = slab[u, idxs[source, 2 * j + 1, first + u]]
                band[pl.ds(at + u * TILE, TILE), j * 128 : (j + 1) * 128] = jnp.where(
                    low_lanes, left, right
                )

    def to_smem(src, number):
        copy = pltpu.make_async_copy(src, idxs.at[number], local_sem.at[3])
        copy.start()
        copy.wait()

    to_smem(idxv, 2)
    own_tiles.wait()

    def place_own(i, carry):
        at = pl.multiple_of((3 + i) * GROUP, GROUP)
        place(tv.at[pl.ds(4 * i, 4)], 2, 4 * i, at)
        return carry

    lax.fori_loop(0, 4, place_own, 0)

    def unpack(v, block, targets):
        for half in range(2):
            rows = pl.ds(block * TILE + half * 32, 32)
            piece = v[:, half * 64 : (half + 1) * 64]
            for ref in targets:
                ref[rows, :] = piece.astype(ref.dtype)

    def one(n, g):
        now, later = n % 2, (n + 1) % 2
        at = g * GROUP if isinstance(g, int) else pl.multiple_of(g * GROUP, GROUP)
        back = (g - 1) * GROUP if isinstance(g, int) else pl.multiple_of((g - 1) * GROUP, GROUP)
        rows = pl.ds(at, GROUP)
        product = jnp.dot(
            band[pl.ds(back, GROUP), :], w[now, pl.ds(back, WIN), :], preferred_element_type=F32
        )
        if n == 0:
            new = (product - 0.1 * y[now, rows, :]) * 0.5
        else:
            new = product - 0.1 * y[now, rows, :] - y[later, rows, :]
        rounded = new.astype(BF)
        if n < 7:
            y[later, rows, :] = new
            w[later, rows, :] = rounded
        return rounded

    for copy in a2a:
        copy.wait_recv()
    vec = both_sides(VEC, xr, xr, hx.at[0], hx.at[1])
    for b in range(OWN):
        unpack(xr[b], OWN + b, (w.at[0], y.at[0]))
    for g in (5, 6):
        one(0, g)

    arrived(vec)
    for side in range(2):

        @pl.when(edges[side])
        def _(side=side):
            for b in range(OWN):
                unpack(hx[side, b], side * 2 * OWN + b, (w.at[0], y.at[0]))

    for n, g in ((0, 4), (0, 7), (1, 5), (1, 6)):
        one(n, g)

    arrived(idx)
    for side in range(2):

        @pl.when(edges[side])
        def _(side=side):
            to_smem(idxh.at[side], side)

    def halo_tiles(n):
        arrived(til[n])
        for side in range(2):

            @pl.when(edges[side])
            def _(side=side):
                place(
                    th.at[side, n], side, 4 * (3 - n) if side == 0 else 4 * n,
                    (2 - n if side == 0 else 7 + n) * GROUP,
                )

    halo_tiles(0)
    for n, g in ((0, 3), (0, 8), (1, 4), (1, 7), (2, 5), (2, 6)):
        one(n, g)
    halo_tiles(1)
    for n, g in ((0, 2), (0, 9), (1, 3), (1, 8), (2, 4), (2, 7)):
        one(n, g)

    for b in range(8):
        op[b] = pack(y[1, pl.ds((20 + b) * TILE, TILE), :]).astype(BF)
    old = both_sides(OLD, op, op, ho.at[0], ho.at[1])

    def pack_group(rounded, dst, first):
        for b in range(4):
            dst[first + b] = pack(rounded[b * TILE : (b + 1) * TILE])

    for slot, g in ((0, 5), (4, 6)):
        pack_group(one(3, g), fp, slot)
    early = both_sides(
        EARLY, fp.at[pl.ds(0, 8)], fp.at[pl.ds(0, 8)], hp.at[0, pl.ds(0, 8)], hp.at[1, pl.ds(0, 8)]
    )
    halo_tiles(2)
    for n, g in ((0, 1), (0, 10), (1, 2), (1, 9), (2, 3), (2, 8)):
        one(n, g)
    for slot, g in ((8, 4), (12, 7)):
        pack_group(one(3, g), fp, slot)
    late = both_sides(
        LATE, fp.at[pl.ds(8, 8)], fp.at[pl.ds(8, 8)], hp.at[0, pl.ds(8, 8)], hp.at[1, pl.ds(8, 8)]
    )
    for g in (5, 6):
        one(4, g)

    arrived(old)
    arrived(early)
    for side in range(2):

        @pl.when(edges[side])
        def _(side=side):
            for b in range(8):
                unpack(hp[side, b], side * 2 * OWN + 4 + b, (w.at[0], y.at[0]))
                unpack(ho[side, b], side * 2 * OWN + 4 + b, (y.at[1],))

    arrived(late)
    for side in range(2):

        @pl.when(edges[side])
        def _(side=side):
            for b in range(8):
                block = b if b < 4 else b + 8
                unpack(hp[side, 8 + b], side * 2 * OWN + block, (w.at[0], y.at[0]))

    for g in (3, 4, 7, 8, 2, 9, 1, 10):
        one(4, g)
    for g in (5, 6, 4, 7, 3, 8, 2, 9):
        one(5, g)
    for g in (5, 6, 4, 7, 3, 8):
        one(6, g)

    quart, gath = [], []
    for i in (2, 1, 3, 0):
        to = lax.rem(zh + i, 4)
        rounded = one(7, 4 + to)
        if i:
            pack_group(rounded, fq.at[to], 0)
            copy = remote(fq.at[to], pc.at[yy, zh], QUART + i, (r, to * 4 + yy))
            copy.start()
            quart.append((i, copy))
        else:
            pack_group(rounded, pc.at[yy, zh], 0)

    def to_y(i):
        piece = pc.at[yy, lax.rem(zh - i + 4, 4)]
        for j in (2, 1, 3):
            device = (r, zh * 4 + lax.rem(yy + j, 4))
            copy = remote(piece, piece, GATH + 4 * i + j, device)
            copy.start()
            gath.append(copy)

    to_y(0)
    for i, copy in (quart[1], quart[2], quart[0]):
        copy.wait_recv()
        to_y(i)

    def assemble(who):
        for half in range(2):
            for b in range(4):
                left, right = pc[who, 2 * half, b], pc[who, 2 * half + 1, b]
                for part in range(2):
                    lanes = slice(part * 64, (part + 1) * 64)
                    fy[2 * who + half, pl.ds(b * TILE + part * 32, 32), :] = jnp.concatenate(
                        [left[:, lanes], right[:, lanes]], axis=1
                    )

    assemble(yy)
    mine = jnp.concatenate(
        [fy[2 * yy + half].astype(F32).T.astype(BF) for half in range(2)], axis=0
    )
    for copy in gath:
        copy.wait_recv()
    for j in range(1, 4):
        assemble(lax.rem(yy + j, 4))

    pair_dev = (r + 1 - 2 * core, c)
    order = (2, 1, 3, 0)
    pairs = {}
    for i in order:
        to = lax.rem(x + i, 4)
        gs[i] = jnp.dot(mine, fy[(1 - core) * 4 + to], preferred_element_type=F32).astype(BF)
        pairs[i] = remote(gs.at[i], gr.at[i], PAIR + i, pair_dev)
        pairs[i].start()
    for i in order:
        gf[i] = jnp.dot(mine, fy[core * 4 + lax.rem(x + i, 4)], preferred_element_type=F32)

    xred = []
    for i in order:
        pairs[i].wait_recv()
        total = gf[i] + gr[i].astype(F32)
        if i:
            to = lax.rem(x + i, 4)
            xsnd[i] = total.astype(BF)
            copy = remote(xsnd.at[i], xrcv.at[i], XRED + i, (zl * 8 + to * 2 + core, c))
            copy.start()
            xred.append((i, copy))

    rows = pl.ds(pl.multiple_of(yy * TILE, TILE), TILE)
    for h in range(4):
        for p in range(2):
            lanes = slice((h % 2) * 64, (h % 2 + 1) * 64)
            out_ref[:, h * 256 + p * 128 : h * 256 + (p + 1) * 128] = jnp.concatenate(
                [fy[4 * p + h // 2, rows, lanes], fy[4 * p + 2 + h // 2, rows, lanes]], axis=1
            )

    for i, copy in xred:
        copy.wait_recv()
        total = total + xrcv[i].astype(F32)
    gf[0] = total
    zs[...] = total.astype(BF)

    zred = []
    for i in (4, 3, 5, 2, 6, 1, 7):
        to = lax.rem(z + i, 8)
        device = (lax.rem(to, 2) * 8 + x * 2 + core, (to // 2) * 4 + yy)
        copy = remote(zs.at[pl.ds(pl.multiple_of(to * 32, 32), 32)], zr.at[i], ZRED + i, device)
        copy.start()
        zred.append((i, copy))
    total = gf[0, pl.ds(pl.multiple_of(z * 32, 32), 32), :]
    for i, copy in zred:
        copy.wait_recv()
        total = total + zr[i].astype(F32)
    ro[r] = (total * SCALE).astype(BF)

    spread = []
    for i in (8, 7, 9, 6, 10, 5, 11, 4, 12, 3, 13, 2, 14, 1, 15):
        copy = remote(ro.at[r], ro.at[r], SPREAD + i, (lax.rem(r + i, 16), c))
        copy.start()
        spread.append(copy)

    for pair in (idx, *til, vec, old, early, late):
        sent(pair)
    for copy in a2a + gath:
        copy.wait_send()
    for i, copy in quart + list(pairs.items()) + xred + zred:
        copy.wait_send()
    for copy in spread:
        copy.wait_recv()
    for l in range(2):
        for h in range(4):
            for p in range(2):
                lanes = slice((h % 2) * 64, (h % 2 + 1) * 64)
                at = [l * 8 + (k * 2 + h // 2) * 2 + p for k in range(2)]
                gram_ref[l * 32 : (l + 1) * 32, h * 256 + p * 128 : h * 256 + (p + 1) * 128] = (
                    jnp.concatenate([ro[at[0]][:, lanes], ro[at[1]][:, lanes]], axis=1).astype(F32)
                )
    for copy in spread:
        copy.wait_send()


def per_device(search_vectors, tile_values, block_columns):
    ext = 12 * GROUP
    return pl.pallas_call(
        kernel,
        out_shape=(
            jax.ShapeDtypeStruct((64, 1024), BF),
            jax.ShapeDtypeStruct((64, 1024), F32),
        ),
        in_specs=[pl.BlockSpec(memory_space=pl.ANY)] * 3,
        out_specs=(pl.BlockSpec(memory_space=pltpu.VMEM), pl.BlockSpec(memory_space=pltpu.VMEM)),
        scratch_shapes=[
            pltpu.VMEM((64, 1024), BF),
            pltpu.VMEM((8, OWN), jnp.int32),
            pltpu.VMEM((16, 32, 128), BF),
            pltpu.VMEM((16, 32, 128), BF),
            pltpu.VMEM((OWN, TILE, 512), BF),
            pltpu.VMEM((2, 3, 4, TILE, 512), BF),
            pltpu.VMEM((16, 128), jnp.int32),
            pltpu.VMEM((2, 16, 128), jnp.int32),
            pltpu.SMEM((3, 16, 128), jnp.int32),
            pltpu.VMEM((4, 9, TILE, 128), BF),
            pltpu.VMEM((10 * GROUP, WIN), BF),
            pltpu.VMEM((2, 16, 32, 128), BF),
            pltpu.VMEM((2, 16, 32, 128), BF),
            pltpu.VMEM((2, 8, 32, 128), BF),
            pltpu.VMEM((2, ext, 64), BF),
            pltpu.VMEM((2, ext, 64), F32),
            pltpu.VMEM((16, 32, 128), BF),
            pltpu.VMEM((8, 32, 128), BF),
            pltpu.VMEM((4, 4, 32, 128), BF),
            pltpu.VMEM((4, 4, 4, 32, 128), BF),
            pltpu.VMEM((8, 256, 128), BF),
            pltpu.VMEM((4, 256, 128), BF),
            pltpu.VMEM((4, 256, 128), BF),
            pltpu.VMEM((4, 256, 128), F32),
            pltpu.VMEM((4, 256, 128), BF),
            pltpu.VMEM((4, 256, 128), BF),
            pltpu.VMEM((256, 128), BF),
            pltpu.VMEM((8, 32, 128), BF),
            pltpu.VMEM((16, 32, 128), BF),
            pltpu.SemaphoreType.DMA((4,)),
            pltpu.SemaphoreType.DMA((COUNT,)),
            pltpu.SemaphoreType.DMA((COUNT,)),
        ],
        compiler_params=pltpu.CompilerParams(
            collective_id=0, has_side_effects=True, vmem_limit_bytes=48 * 1024 * 1024
        ),
        name="filter_and_gram",
    )(*(pltpu.with_memory_space_constraint(v, pltpu.HBM) for v in (search_vectors, block_columns.T, tile_values)))


def solution(mesh):
    return jax.shard_map(
        per_device,
        mesh=mesh,
        in_specs=(P(("rows", "cols"), None), P("rows", None, None), P("rows", None)),
        out_specs=(P(("rows", "cols"), None), P("cols", None)),
        check_vma=False,
    )
```

```python
import jax
import jax.numpy as jnp
from jax import lax
from jax.experimental import pallas as pl
from jax.experimental.pallas import tpu as pltpu
from jax.sharding import PartitionSpec as P

MESH = pl.DeviceIdType.MESH
BF, F32 = jnp.bfloat16, jnp.float32

TILE = 64
OWN = 16
GROUP = 256
WIN = 768
SCALE = 1.0 / 16384

A2A, TIL, IDX, VEC, EARLY, OLD, LATE = 0, 16, 22, 24, 26, 28, 30
QUART, GATH, PAIR, XRED, ZRED, SPREAD, COUNT = 32, 36, 52, 56, 60, 68, 84


def swap(v):
    return jnp.concatenate([v[:, 64:], v[:, :64]], axis=1)


def pack(block):
    return jnp.concatenate([block[:32], block[32:]], axis=1)


def kernel(
    x_hbm, cols_hbm, tiles_hbm, out_ref, gram_ref,
    x_ref, cols_ref, xs, xr, tv, th, idxv, idxh, idxs, slab, band, hx, hp, ho, w, y,
    fp, op, fq, pc, fy, gs, gr, gf, xsnd, xrcv, zs, zr, ro, local_sem, ss, rs,
):
    r, c = lax.axis_index("rows"), lax.axis_index("cols")
    yy, zh = lax.rem(c, 4), c // 4
    core, x, zl = lax.rem(r, 2), lax.rem(r // 2, 4), r // 8
    z = zh * 2 + zl

    def remote(src, dst, number, device):
        return pltpu.make_async_remote_copy(
            src_ref=src, dst_ref=dst, send_sem=ss.at[number], recv_sem=rs.at[number],
            device_id=device, device_id_type=MESH,
        )

    own_x = pltpu.make_async_copy(x_hbm, x_ref, local_sem.at[0])
    own_cols = pltpu.make_async_copy(cols_hbm, cols_ref, local_sem.at[1])
    own_tiles = pltpu.make_async_copy(tiles_hbm, tv, local_sem.at[2])

    barrier = pltpu.get_barrier_semaphore()

    def greet(device):
        pl.semaphore_signal(barrier, inc=1, device_id=device, device_id_type=MESH)

    for i in (8, 7, 9, 6, 10, 5, 11, 4, 12, 3, 13, 2, 14, 1, 15):
        greet((r, lax.rem(c + i, 16)))
        greet((lax.rem(r + i, 16), c))
    for i in range(1, 4):
        greet((lax.rem(r + 8, 16), lax.rem(zh + i, 4) * 4 + yy))
    at_7, at_8 = r == 7, r == 8
    middle = jnp.logical_or(at_7, at_8)
    turned = jnp.where(at_7, lax.rem(zh + 3, 4), lax.rem(zh + 1, 4)) * 4 + yy
    pl.when(middle)(lambda: greet((15 - r, turned)))
    own_x.start()
    own_cols.start()
    own_tiles.start()

    has_low, has_high = r > 0, r < 15
    edges = (has_low, has_high)
    up, down = jnp.minimum(r + 1, 15), jnp.maximum(r - 1, 0)

    def zero(ref, first, count):
        ref[pl.ds(first, count), :] = jnp.zeros((count, ref.shape[1]), ref.dtype)

    for side in range(2):

        @pl.when(jnp.logical_not(edges[side]))
        def _(side=side):
            zero(band, 7 * side * GROUP, 3 * GROUP)
            zero(w.at[0], side * 8 * GROUP, 4 * GROUP)

    for u in range(4):
        slab[u, 8] = jnp.zeros((TILE, 128), BF)

    own_x.wait()
    for g in range(16):
        xs[g] = pack(x_ref[:, g * 64 : (g + 1) * 64])

    own_cols.wait()
    slot = lax.broadcasted_iota(jnp.int32, (16, OWN), 0)
    first_col = r * OWN + (lax.broadcasted_iota(jnp.int32, (8, OWN), 1) // 4) * 4 - 4
    places = cols_ref[...] - first_col
    slabs = jnp.full((16, OWN), 8, jnp.int32)
    for k in range(8):
        which = jnp.where(lax.rem(slot, 2) == 0, k, k + 1 - 2 * (k % 2))
        slabs = jnp.where(slot == places[k : k + 1, :], which, slabs)
    idxv[...] = jnp.zeros_like(idxv)
    idxv[:, :OWN] = slabs

    pl.when(middle)(lambda: pl.semaphore_wait(barrier, 34))
    pl.when(jnp.logical_not(middle))(lambda: pl.semaphore_wait(barrier, 33))

    a2a = []
    for i in (8, 7, 9, 6, 10, 5, 11, 4, 12, 3, 13, 2, 14, 1, 15):
        to = lax.rem(c + i, 16)
        copy = remote(xs.at[to], xr.at[c], A2A + i, (r, to))
        copy.start()
        a2a.append(copy)

    def both_sides(number, to_up, to_down, low_dst, high_dst, col_up=c, col_down=c):
        a = remote(to_up, low_dst, number, (up, col_up))
        b = remote(to_down, high_dst, number + 1, (down, col_down))
        pl.when(has_high)(a.start)
        pl.when(has_low)(b.start)
        return a, b

    def arrived(pair):
        pl.when(has_low)(pair[0].wait_recv)
        pl.when(has_high)(pair[1].wait_recv)

    def sent(pair):
        pl.when(has_high)(pair[0].wait_send)
        pl.when(has_low)(pair[1].wait_send)

    idx = both_sides(IDX, idxv, idxv, idxh.at[0], idxh.at[1])
    til = [
        both_sides(
            TIL + 2 * n, tiles_hbm.at[pl.ds(4 * (3 - n), 4)], tiles_hbm.at[pl.ds(4 * n, 4)],
            th.at[0, n], th.at[1, n],
            *((jnp.where(at_7, turned, c), jnp.where(at_8, turned, c)) if n == 1 else (c, c)),
        )
        for n in range(3)
    ]
    xr[c] = xs[c]

    low_lanes = lax.broadcasted_iota(jnp.int32, (TILE, 128), 1) < 64

    def place(tiles, source, first, at):
        for u in range(4):
            for p in range(4):
                piece = tiles[u, :, p * 128 : (p + 1) * 128]
                slab[u, 2 * p] = piece
                slab[u, 2 * p + 1] = swap(piece)
            for j in range(6):
                left = slab[u, idxs[source, 2 * j, first + u]]
                right = slab[u, idxs[source, 2 * j + 1, first + u]]
                band[pl.ds(at + u * TILE, TILE), j * 128 : (j + 1) * 128] = jnp.where(
                    low_lanes, left, right
                )

    def to_smem(src, number):
        copy = pltpu.make_async_copy(src, idxs.at[number], local_sem.at[3])
        copy.start()
        copy.wait()

    to_smem(idxv, 2)
    own_tiles.wait()

    def place_own(i, carry):
        at = pl.multiple_of((3 + i) * GROUP, GROUP)
        place(tv.at[pl.ds(4 * i, 4)], 2, 4 * i, at)
        return carry

    lax.fori_loop(0, 4, place_own, 0)

    def unpack(v, block, ref):
        for half in range(2):
            rows = pl.ds(block * TILE + half * 32, 32)
            ref[rows, :] = v[:, half * 64 : (half + 1) * 64].astype(ref.dtype)

    def one(n, g):
        now, later = n % 2, (n + 1) % 2
        at = g * GROUP if isinstance(g, int) else pl.multiple_of(g * GROUP, GROUP)
        back = (g - 1) * GROUP if isinstance(g, int) else pl.multiple_of((g - 1) * GROUP, GROUP)
        rows = pl.ds(at, GROUP)
        product = jnp.dot(
            band[pl.ds(back, GROUP), :], w[now, pl.ds(back, WIN), :], preferred_element_type=F32
        )
        outer = n in (4, 5) and not 4 <= g <= 7
        current = w[now, rows, :].astype(F32) if n == 0 or (n == 4 and outer) else y[now, rows, :]
        if n == 0:
            new = (product - 0.1 * current) * 0.5
        else:
            before = w if n == 1 or (n == 5 and outer) else y
            new = product - 0.1 * current - before[later, rows, :].astype(F32)
        rounded = new.astype(BF)
        if n < 7:
            y[later, rows, :] = new
            w[later, rows, :] = rounded
        return rounded

    for copy in a2a:
        copy.wait_recv()
    vec = both_sides(VEC, xr, xr, hx.at[0], hx.at[1])
    for b in range(OWN):
        unpack(xr[b], OWN + b, w.at[0])
    for g in (5, 6):
        one(0, g)

    arrived(idx)
    for side in range(2):

        @pl.when(edges[side])
        def _(side=side):
            to_smem(idxh.at[side], side)

    def halo_tiles(n):
        arrived(til[n])
        for side in range(2):

            @pl.when(edges[side])
            def _(side=side):
                place(
                    th.at[side, n], side, 4 * (3 - n) if side == 0 else 4 * n,
                    (2 - n if side == 0 else 7 + n) * GROUP,
                )

    halo_tiles(0)
    halo_tiles(1)

    arrived(vec)
    for side in range(2):

        @pl.when(edges[side])
        def _(side=side):
            for b in range(OWN):
                unpack(hx[side, b], side * 2 * OWN + b, w.at[0])

    for g in (4, 7, 3, 8, 2, 9):
        one(0, g)
    for g in (5, 6, 4, 7, 3, 8):
        one(1, g)
    for g in (5, 6, 4, 7):
        one(2, g)

    for b in range(8):
        op[b] = pack(y[1, pl.ds((20 + b) * TILE, TILE), :]).astype(BF)
    old = both_sides(OLD, op, op, ho.at[0], ho.at[1])

    def pack_group(rounded, dst, first):
        for b in range(4):
            dst[first + b] = pack(rounded[b * TILE : (b + 1) * TILE])

    for slot, g in ((0, 5), (4, 6)):
        pack_group(one(3, g), fp, slot)
    early = both_sides(
        EARLY, fp.at[pl.ds(0, 8)], fp.at[pl.ds(0, 8)], hp.at[0, pl.ds(0, 8)], hp.at[1, pl.ds(0, 8)]
    )
    halo_tiles(2)
    for n, g in ((0, 1), (0, 10), (1, 2), (1, 9), (2, 3), (2, 8)):
        one(n, g)
    for slot, g in ((8, 4), (12, 7)):
        pack_group(one(3, g), fp, slot)
    late = both_sides(
        LATE, fp.at[pl.ds(8, 8)], fp.at[pl.ds(8, 8)], hp.at[0, pl.ds(8, 8)], hp.at[1, pl.ds(8, 8)]
    )
    for g in (5, 6):
        one(4, g)

    arrived(old)
    arrived(early)
    for side in range(2):

        @pl.when(edges[side])
        def _(side=side):
            for b in range(8):
                unpack(hp[side, b], side * 2 * OWN + 4 + b, w.at[0])
                unpack(ho[side, b], side * 2 * OWN + 4 + b, y.at[1])

    arrived(late)
    for side in range(2):

        @pl.when(edges[side])
        def _(side=side):
            for b in range(8):
                block = b if b < 4 else b + 8
                unpack(hp[side, 8 + b], side * 2 * OWN + block, w.at[0])

    for g in (3, 4, 7, 8, 2, 9, 1, 10):
        one(4, g)
    for g in (5, 6, 4, 7, 3, 8, 2, 9):
        one(5, g)
    for g in (5, 6, 4, 7, 3, 8):
        one(6, g)

    quart, gath = [], []
    for i in (2, 1, 3, 0):
        to = lax.rem(zh + i, 4)
        rounded = one(7, 4 + to)
        if i:
            pack_group(rounded, fq.at[to], 0)
            copy = remote(fq.at[to], pc.at[yy, zh], QUART + i, (r, to * 4 + yy))
            copy.start()
            quart.append((i, copy))
        else:
            pack_group(rounded, pc.at[yy, zh], 0)

    def to_y(i):
        piece = pc.at[yy, lax.rem(zh - i + 4, 4)]
        for j in (2, 1, 3):
            device = (r, zh * 4 + lax.rem(yy + j, 4))
            copy = remote(piece, piece, GATH + 4 * i + j, device)
            copy.start()
            gath.append(copy)

    to_y(0)
    for i, copy in (quart[1], quart[2], quart[0]):
        copy.wait_recv()
        to_y(i)

    def assemble(who):
        for half in range(2):
            for b in range(4):
                left, right = pc[who, 2 * half, b], pc[who, 2 * half + 1, b]
                for part in range(2):
                    lanes = slice(part * 64, (part + 1) * 64)
                    fy[2 * who + half, pl.ds(b * TILE + part * 32, 32), :] = jnp.concatenate(
                        [left[:, lanes], right[:, lanes]], axis=1
                    )

    assemble(yy)
    mine = jnp.concatenate(
        [fy[2 * yy + half].astype(F32).T.astype(BF) for half in range(2)], axis=0
    )
    for copy in gath:
        copy.wait_recv()
    for j in range(1, 4):
        assemble(lax.rem(yy + j, 4))

    pair_dev = (r + 1 - 2 * core, c)
    order = (2, 1, 3, 0)
    pairs = {}
    for i in order:
        to = lax.rem(x + i, 4)
        gs[i] = jnp.dot(mine, fy[(1 - core) * 4 + to], preferred_element_type=F32).astype(BF)
        pairs[i] = remote(gs.at[i], gr.at[i], PAIR + i, pair_dev)
        pairs[i].start()
    for i in order:
        gf[i] = jnp.dot(mine, fy[core * 4 + lax.rem(x + i, 4)], preferred_element_type=F32)

    xred = []
    for i in order:
        pairs[i].wait_recv()
        total = gf[i] + gr[i].astype(F32)
        if i:
            to = lax.rem(x + i, 4)
            xsnd[i] = total.astype(BF)
            copy = remote(xsnd.at[i], xrcv.at[i], XRED + i, (zl * 8 + to * 2 + core, c))
            copy.start()
            xred.append((i, copy))

    rows = pl.ds(pl.multiple_of(yy * TILE, TILE), TILE)
    for h in range(4):
        for p in range(2):
            lanes = slice((h % 2) * 64, (h % 2 + 1) * 64)
            out_ref[:, h * 256 + p * 128 : h * 256 + (p + 1) * 128] = jnp.concatenate(
                [fy[4 * p + h // 2, rows, lanes], fy[4 * p + 2 + h // 2, rows, lanes]], axis=1
            )

    for i, copy in xred:
        copy.wait_recv()
        total = total + xrcv[i].astype(F32)
    gf[0] = total
    zs[...] = total.astype(BF)

    zred = []
    for i in (4, 3, 5, 2, 6, 1, 7):
        to = lax.rem(z + i, 8)
        device = (lax.rem(to, 2) * 8 + x * 2 + core, (to // 2) * 4 + yy)
        copy = remote(zs.at[pl.ds(pl.multiple_of(to * 32, 32), 32)], zr.at[i], ZRED + i, device)
        copy.start()
        zred.append((i, copy))
    total = gf[0, pl.ds(pl.multiple_of(z * 32, 32), 32), :]
    for i, copy in zred:
        copy.wait_recv()
        total = total + zr[i].astype(F32)
    ro[r] = (total * SCALE).astype(BF)

    spread = []
    for i in (12, 11, 13, 10, 14, 4, 3, 5, 9, 15, 2, 6, 7, 8, 1):
        copy = remote(ro.at[r], ro.at[r], SPREAD + i, (lax.rem(r + i, 16), c))
        copy.start()
        spread.append(copy)

    for pair in (idx, *til, vec, old, early, late):
        sent(pair)
    for copy in a2a + gath:
        copy.wait_send()
    for i, copy in quart + list(pairs.items()) + xred + zred:
        copy.wait_send()
    for copy in spread:
        copy.wait_recv()
    for l in range(2):
        for h in range(4):
            for p in range(2):
                lanes = slice((h % 2) * 64, (h % 2 + 1) * 64)
                at = [l * 8 + (k * 2 + h // 2) * 2 + p for k in range(2)]
                gram_ref[l * 32 : (l + 1) * 32, h * 256 + p * 128 : h * 256 + (p + 1) * 128] = (
                    jnp.concatenate([ro[at[0]][:, lanes], ro[at[1]][:, lanes]], axis=1).astype(F32)
                )
    for copy in spread:
        copy.wait_send()


def per_device(search_vectors, tile_values, block_columns):
    ext = 12 * GROUP
    return pl.pallas_call(
        kernel,
        out_shape=(
            jax.ShapeDtypeStruct((64, 1024), BF),
            jax.ShapeDtypeStruct((64, 1024), F32),
        ),
        in_specs=[pl.BlockSpec(memory_space=pl.ANY)] * 3,
        out_specs=(pl.BlockSpec(memory_space=pltpu.VMEM), pl.BlockSpec(memory_space=pltpu.VMEM)),
        scratch_shapes=[
            pltpu.VMEM((64, 1024), BF),
            pltpu.VMEM((8, OWN), jnp.int32),
            pltpu.VMEM((16, 32, 128), BF),
            pltpu.VMEM((16, 32, 128), BF),
            pltpu.VMEM((OWN, TILE, 512), BF),
            pltpu.VMEM((2, 3, 4, TILE, 512), BF),
            pltpu.VMEM((16, 128), jnp.int32),
            pltpu.VMEM((2, 16, 128), jnp.int32),
            pltpu.SMEM((3, 16, 128), jnp.int32),
            pltpu.VMEM((4, 9, TILE, 128), BF),
            pltpu.VMEM((10 * GROUP, WIN), BF),
            pltpu.VMEM((2, 16, 32, 128), BF),
            pltpu.VMEM((2, 16, 32, 128), BF),
            pltpu.VMEM((2, 8, 32, 128), BF),
            pltpu.VMEM((2, ext, 64), BF),
            pltpu.VMEM((2, ext, 64), F32),
            pltpu.VMEM((16, 32, 128), BF),
            pltpu.VMEM((8, 32, 128), BF),
            pltpu.VMEM((4, 4, 32, 128), BF),
            pltpu.VMEM((4, 4, 4, 32, 128), BF),
            pltpu.VMEM((8, 256, 128), BF),
            pltpu.VMEM((4, 256, 128), BF),
            pltpu.VMEM((4, 256, 128), BF),
            pltpu.VMEM((4, 256, 128), F32),
            pltpu.VMEM((4, 256, 128), BF),
            pltpu.VMEM((4, 256, 128), BF),
            pltpu.VMEM((256, 128), BF),
            pltpu.VMEM((8, 32, 128), BF),
            pltpu.VMEM((16, 32, 128), BF),
            pltpu.SemaphoreType.DMA((4,)),
            pltpu.SemaphoreType.DMA((COUNT,)),
            pltpu.SemaphoreType.DMA((COUNT,)),
        ],
        compiler_params=pltpu.CompilerParams(
            collective_id=0, has_side_effects=True, vmem_limit_bytes=48 * 1024 * 1024
        ),
        name="filter_and_gram",
    )(*(pltpu.with_memory_space_constraint(v, pltpu.HBM) for v in (search_vectors, block_columns.T, tile_values)))


def solution(mesh):
    return jax.shard_map(
        per_device,
        mesh=mesh,
        in_specs=(P(("rows", "cols"), None), P("rows", None, None), P("rows", None)),
        out_specs=(P(("rows", "cols"), None), P("cols", None)),
        check_vma=False,
    )
```

```python
import jax
import jax.numpy as jnp
from jax import lax
from jax.experimental import pallas as pl
from jax.experimental.pallas import tpu as pltpu
from jax.sharding import PartitionSpec as P

MESH = pl.DeviceIdType.MESH
BF, F32 = jnp.bfloat16, jnp.float32

TILE = 64
OWN = 16
GROUP = 256
WIN = 768
SCALE = 1.0 / 16384

A2A, TIL, IDX, VEC, EARLY, OLD, LATE = 0, 16, 22, 24, 26, 28, 30
QUART, GATH, PAIR, XRED, ZRED, SPREAD, RELAY, COUNT = 32, 36, 52, 56, 72, 80, 88, 96


def swap(v):
    return jnp.concatenate([v[:, 64:], v[:, :64]], axis=1)


def pack(block):
    return jnp.concatenate([block[:32], block[32:]], axis=1)


def kernel(
    x_hbm, cols_hbm, tiles_hbm, out_ref, gram_ref,
    x_ref, cols_ref, xs, xr, tv, th, idxv, idxh, idxs, slab, band, hx, hp, ho, w, y,
    fp, op, fq, pc, fy, gs, gr, gf, xsnd, xrcv, zs, zr, ro, local_sem, ss, rs,
):
    r, c = lax.axis_index("rows"), lax.axis_index("cols")
    yy, zh = lax.rem(c, 4), c // 4
    core, x, zl = lax.rem(r, 2), lax.rem(r // 2, 4), r // 8
    z = zh * 2 + zl

    def remote(src, dst, number, device):
        return pltpu.make_async_remote_copy(
            src_ref=src, dst_ref=dst, send_sem=ss.at[number], recv_sem=rs.at[number],
            device_id=device, device_id_type=MESH,
        )

    own_x = pltpu.make_async_copy(x_hbm, x_ref, local_sem.at[0])
    own_cols = pltpu.make_async_copy(cols_hbm, cols_ref, local_sem.at[1])
    own_tiles = pltpu.make_async_copy(tiles_hbm, tv, local_sem.at[2])

    barrier = pltpu.get_barrier_semaphore()

    def greet(device):
        pl.semaphore_signal(barrier, inc=1, device_id=device, device_id_type=MESH)

    for i in (8, 7, 9, 6, 10, 5, 11, 4, 12, 3, 13, 2, 14, 1, 15):
        greet((r, lax.rem(c + i, 16)))
    for i in range(4):
        greet((lax.rem(r + 8, 16), lax.rem(zh + i, 4) * 4 + yy))
    for i in range(1, 8):
        greet((zl * 8 + lax.rem(r + i, 8), c))
    at_7, at_8 = r == 7, r == 8
    middle = jnp.logical_or(at_7, at_8)
    turned = jnp.where(at_7, lax.rem(zh + 3, 4), lax.rem(zh + 1, 4)) * 4 + yy
    @pl.when(middle)
    def _():
        greet((15 - r, c))
        greet((15 - r, turned))

    own_x.start()
    own_cols.start()
    own_tiles.start()

    has_low, has_high = r > 0, r < 15
    edges = (has_low, has_high)
    up, down = jnp.minimum(r + 1, 15), jnp.maximum(r - 1, 0)

    def zero(ref, first, count):
        ref[pl.ds(first, count), :] = jnp.zeros((count, ref.shape[1]), ref.dtype)

    for side in range(2):

        @pl.when(jnp.logical_not(edges[side]))
        def _(side=side):
            zero(band, 7 * side * GROUP, 3 * GROUP)
            zero(w.at[0], side * 8 * GROUP, 4 * GROUP)

    for u in range(4):
        slab[u, 8] = jnp.zeros((TILE, 128), BF)

    own_x.wait()
    for g in range(16):
        xs[g] = pack(x_ref[:, g * 64 : (g + 1) * 64])

    own_cols.wait()
    slot = lax.broadcasted_iota(jnp.int32, (16, OWN), 0)
    first_col = r * OWN + (lax.broadcasted_iota(jnp.int32, (8, OWN), 1) // 4) * 4 - 4
    places = cols_ref[...] - first_col
    slabs = jnp.full((16, OWN), 8, jnp.int32)
    for k in range(8):
        which = jnp.where(lax.rem(slot, 2) == 0, k, k + 1 - 2 * (k % 2))
        slabs = jnp.where(slot == places[k : k + 1, :], which, slabs)
    idxv[...] = jnp.zeros_like(idxv)
    idxv[:, :OWN] = slabs

    pl.when(middle)(lambda: pl.semaphore_wait(barrier, 28))
    pl.when(jnp.logical_not(middle))(lambda: pl.semaphore_wait(barrier, 26))

    a2a = []
    for i in (8, 7, 9, 6, 10, 5, 11, 4, 12, 3, 13, 2, 14, 1, 15):
        to = lax.rem(c + i, 16)
        copy = remote(xs.at[to], xr.at[c], A2A + i, (r, to))
        copy.start()
        a2a.append(copy)

    def both_sides(number, to_up, to_down, low_dst, high_dst, col_up=c, col_down=c):
        a = remote(to_up, low_dst, number, (up, col_up))
        b = remote(to_down, high_dst, number + 1, (down, col_down))
        pl.when(has_high)(a.start)
        pl.when(has_low)(b.start)
        return a, b

    def arrived(pair):
        pl.when(has_low)(pair[0].wait_recv)
        pl.when(has_high)(pair[1].wait_recv)

    def sent(pair):
        pl.when(has_high)(pair[0].wait_send)
        pl.when(has_low)(pair[1].wait_send)

    idx = both_sides(IDX, idxv, idxv, idxh.at[0], idxh.at[1])
    mine_of = [th.at[side, 2, pl.ds(yy, 1)] for side in range(2)]
    far = both_sides(
        TIL + 4, tiles_hbm.at[pl.ds(4 + yy, 1)], tiles_hbm.at[pl.ds(8 + yy, 1)], *mine_of
    )
    til = [
        both_sides(
            TIL + 2 * n, tiles_hbm.at[pl.ds(4 * (3 - n), 4)], tiles_hbm.at[pl.ds(4 * n, 4)],
            th.at[0, n], th.at[1, n],
            *((jnp.where(at_7, turned, c), jnp.where(at_8, turned, c)) if n == 1 else (c, c)),
        )
        for n in range(2)
    ]
    relay = [
        [
            remote(v, v, RELAY + 4 * side + j, (r, zh * 4 + lax.rem(yy + j, 4)))
            for j in (2, 1, 3)
        ]
        for side, v in enumerate(mine_of)
    ]

    def on_side(side, method):
        @pl.when(edges[side])
        def _():
            for copy in relay[side]:
                getattr(copy, method)()

    xr[c] = xs[c]

    low_lanes = lax.broadcasted_iota(jnp.int32, (TILE, 128), 1) < 64

    def place(tiles, source, first, at):
        for u in range(4):
            for p in range(4):
                piece = tiles[u, :, p * 128 : (p + 1) * 128]
                slab[u, 2 * p] = piece
                slab[u, 2 * p + 1] = swap(piece)
            for j in range(6):
                left = slab[u, idxs[source, 2 * j, first + u]]
                right = slab[u, idxs[source, 2 * j + 1, first + u]]
                band[pl.ds(at + u * TILE, TILE), j * 128 : (j + 1) * 128] = jnp.where(
                    low_lanes, left, right
                )

    def to_smem(src, number):
        copy = pltpu.make_async_copy(src, idxs.at[number], local_sem.at[3])
        copy.start()
        copy.wait()

    to_smem(idxv, 2)
    own_tiles.wait()

    def place_own(i, carry):
        at = pl.multiple_of((3 + i) * GROUP, GROUP)
        place(tv.at[pl.ds(4 * i, 4)], 2, 4 * i, at)
        return carry

    lax.fori_loop(0, 4, place_own, 0)
    arrived(far)
    for side in range(2):
        on_side(side, "start")

    def unpack(v, block, ref):
        for half in range(2):
            rows = pl.ds(block * TILE + half * 32, 32)
            ref[rows, :] = v[:, half * 64 : (half + 1) * 64].astype(ref.dtype)

    def one(n, g):
        now, later = n % 2, (n + 1) % 2
        at = g * GROUP if isinstance(g, int) else pl.multiple_of(g * GROUP, GROUP)
        back = (g - 1) * GROUP if isinstance(g, int) else pl.multiple_of((g - 1) * GROUP, GROUP)
        rows = pl.ds(at, GROUP)
        product = jnp.dot(
            band[pl.ds(back, GROUP), :], w[now, pl.ds(back, WIN), :], preferred_element_type=F32
        )
        outer = n in (4, 5) and not 4 <= g <= 7
        current = w[now, rows, :].astype(F32) if n == 0 or (n == 4 and outer) else y[now, rows, :]
        if n == 0:
            new = (product - 0.1 * current) * 0.5
        else:
            before = w if n == 1 or (n == 5 and outer) else y
            new = product - 0.1 * current - before[later, rows, :].astype(F32)
        rounded = new.astype(BF)
        if n < 7:
            y[later, rows, :] = new
            w[later, rows, :] = rounded
        return rounded

    for copy in a2a:
        copy.wait_recv()
    vec = both_sides(VEC, xr, xr, hx.at[0], hx.at[1])
    for b in range(OWN):
        unpack(xr[b], OWN + b, w.at[0])
    for g in (5, 6):
        one(0, g)

    arrived(idx)
    for side in range(2):

        @pl.when(edges[side])
        def _(side=side):
            to_smem(idxh.at[side], side)

    def halo_tiles(n):
        if n < 2:
            arrived(til[n])
        for side in range(2):
            if n == 2:
                on_side(side, "wait_recv")

            @pl.when(edges[side])
            def _(side=side):
                place(
                    th.at[side, n], side, 4 * (3 - n) if side == 0 else 4 * n,
                    (2 - n if side == 0 else 7 + n) * GROUP,
                )

    halo_tiles(0)
    halo_tiles(1)

    arrived(vec)
    for side in range(2):

        @pl.when(edges[side])
        def _(side=side):
            for b in range(OWN):
                unpack(hx[side, b], side * 2 * OWN + b, w.at[0])

    for g in (4, 7, 3, 8, 2, 9):
        one(0, g)
    for g in (5, 6, 4, 7, 3, 8):
        one(1, g)
    for g in (5, 6, 4, 7):
        one(2, g)

    for b in range(8):
        op[b] = pack(y[1, pl.ds((20 + b) * TILE, TILE), :]).astype(BF)
    old = both_sides(OLD, op, op, ho.at[0], ho.at[1])

    def pack_group(rounded, dst, first):
        for b in range(4):
            dst[first + b] = pack(rounded[b * TILE : (b + 1) * TILE])

    for slot, g in ((0, 5), (4, 6)):
        pack_group(one(3, g), fp, slot)
    early = both_sides(
        EARLY, fp.at[pl.ds(0, 8)], fp.at[pl.ds(0, 8)], hp.at[0, pl.ds(0, 8)], hp.at[1, pl.ds(0, 8)]
    )
    halo_tiles(2)
    for n, g in ((0, 1), (0, 10), (1, 2), (1, 9), (2, 3), (2, 8)):
        one(n, g)
    for slot, g in ((8, 4), (12, 7)):
        pack_group(one(3, g), fp, slot)
    late = both_sides(
        LATE, fp.at[pl.ds(8, 8)], fp.at[pl.ds(8, 8)], hp.at[0, pl.ds(8, 8)], hp.at[1, pl.ds(8, 8)]
    )
    for g in (5, 6):
        one(4, g)

    arrived(old)
    arrived(early)
    for side in range(2):

        @pl.when(edges[side])
        def _(side=side):
            for b in range(8):
                unpack(hp[side, b], side * 2 * OWN + 4 + b, w.at[0])
                unpack(ho[side, b], side * 2 * OWN + 4 + b, y.at[1])

    arrived(late)
    for side in range(2):

        @pl.when(edges[side])
        def _(side=side):
            for b in range(8):
                block = b if b < 4 else b + 8
                unpack(hp[side, 8 + b], side * 2 * OWN + block, w.at[0])

    for g in (3, 4, 7, 8, 2, 9, 1, 10):
        one(4, g)
    for g in (5, 6, 4, 7, 3, 8, 2, 9):
        one(5, g)
    for g in (5, 6, 4, 7, 3, 8):
        one(6, g)

    quart, gath = [], []
    for i in (2, 1, 3, 0):
        to = lax.rem(zh + i, 4)
        rounded = one(7, 4 + to)
        if i:
            pack_group(rounded, fq.at[to], 0)
            copy = remote(fq.at[to], pc.at[yy, zh], QUART + i, (r, to * 4 + yy))
            copy.start()
            quart.append((i, copy))
        else:
            pack_group(rounded, pc.at[yy, zh], 0)

    def to_y(i):
        piece = pc.at[yy, lax.rem(zh - i + 4, 4)]
        for j in (2, 1, 3):
            device = (r, zh * 4 + lax.rem(yy + j, 4))
            copy = remote(piece, piece, GATH + 4 * i + j, device)
            copy.start()
            gath.append(copy)

    to_y(0)
    for i, copy in (quart[1], quart[2], quart[0]):
        copy.wait_recv()
        to_y(i)

    def assemble(who):
        for half in range(2):
            for b in range(4):
                left, right = pc[who, 2 * half, b], pc[who, 2 * half + 1, b]
                for part in range(2):
                    lanes = slice(part * 64, (part + 1) * 64)
                    fy[2 * who + half, pl.ds(b * TILE + part * 32, 32), :] = jnp.concatenate(
                        [left[:, lanes], right[:, lanes]], axis=1
                    )

    assemble(yy)
    mine = jnp.concatenate(
        [fy[2 * yy + half].astype(F32).T.astype(BF) for half in range(2)], axis=0
    )
    for copy in gath:
        copy.wait_recv()
    for j in range(1, 4):
        assemble(lax.rem(yy + j, 4))

    pair_dev = (r + 1 - 2 * core, c)
    order = (2, 1, 3, 0)
    pairs = {}
    for i in order:
        to = lax.rem(x + i, 4)
        gs[i] = jnp.dot(mine, fy[(1 - core) * 4 + to], preferred_element_type=F32).astype(BF)
        pairs[i] = remote(gs.at[i], gr.at[i], PAIR + i, pair_dev)
        pairs[i].start()
    for i in order:
        gf[i] = jnp.dot(mine, fy[core * 4 + lax.rem(x + i, 4)], preferred_element_type=F32)

    xred = {}
    parts = [lax.rem(zh + d, 4) for d in (2, 1, 3, 0)]
    for i in order:
        pairs[i].wait_recv()
        total = gf[i] + gr[i].astype(F32)
        if i:
            xsnd[i] = total.astype(BF)
        else:
            gf[0] = total
    for k, part in enumerate(parts):
        rows = pl.ds(pl.multiple_of(part * 64, 64), 64)
        for i in order[:3]:
            device = (zl * 8 + lax.rem(x + i, 4) * 2 + core, c)
            xred[i, k] = remote(xsnd.at[i, rows], xrcv.at[i, rows], XRED + 4 * i + k, device)
            xred[i, k].start()

    rows = pl.ds(pl.multiple_of(yy * TILE, TILE), TILE)
    for h in range(4):
        for p in range(2):
            lanes = slice((h % 2) * 64, (h % 2 + 1) * 64)
            out_ref[:, h * 256 + p * 128 : h * 256 + (p + 1) * 128] = jnp.concatenate(
                [fy[4 * p + h // 2, rows, lanes], fy[4 * p + 2 + h // 2, rows, lanes]], axis=1
            )

    for k, part in enumerate(parts):
        rows = pl.ds(pl.multiple_of(part * 64, 64), 64)
        total = gf[0, rows, :]
        for i in order[:3]:
            xred[i, k].wait_recv()
            total = total + xrcv[i, rows, :].astype(F32)
        zs[rows, :] = total.astype(BF)
        for lo in (zl, 1 - zl) if k < 3 else (1 - zl,):
            i = lax.rem(part * 2 + lo - z + 8, 8)
            copy = remote(zs.at[rows], zr.at[z], ZRED + i, (lo * 8 + x * 2 + core, part * 4 + yy))
            copy.start()
    zr[z] = zs[pl.ds(pl.multiple_of(zh * 64, 64), 64), :]
    landed = [remote(zs.at[pl.ds(0, 64)], zr.at[z], ZRED + i, pair_dev) for i in range(1, 8)]
    for copy in landed:
        copy.wait_recv()
    total = zr[0].astype(F32)
    for i in range(1, 8):
        total = total + zr[i].astype(F32)
    rr = lax.rem(r, 8)
    ro[rr] = (total * SCALE).astype(BF)

    spread = []
    for i in (4, 3, 5, 2, 6, 7, 1):
        copy = remote(ro.at[rr], ro.at[rr], SPREAD + i, (zl * 8 + lax.rem(rr + i, 8), c))
        copy.start()
        spread.append(copy)

    for side in range(2):
        on_side(side, "wait_send")
    for pair in (idx, far, *til, vec, old, early, late):
        sent(pair)
    for copy in a2a + gath:
        copy.wait_send()
    for i, copy in quart + list(pairs.items()):
        copy.wait_send()
    for copy in list(xred.values()) + landed:
        copy.wait_send()
    for copy in spread:
        copy.wait_recv()
    for h in range(4):
        for p in range(2):
            lanes = slice((h % 2) * 64, (h % 2 + 1) * 64)
            at = [(k * 2 + h // 2) * 2 + p for k in range(2)]
            gram_ref[:, h * 256 + p * 128 : h * 256 + (p + 1) * 128] = jnp.concatenate(
                [ro[at[0]][:, lanes], ro[at[1]][:, lanes]], axis=1
            ).astype(F32)
    for copy in spread:
        copy.wait_send()


def per_device(search_vectors, tile_values, block_columns):
    ext = 12 * GROUP
    return pl.pallas_call(
        kernel,
        out_shape=(
            jax.ShapeDtypeStruct((64, 1024), BF),
            jax.ShapeDtypeStruct((64, 1024), F32),
        ),
        in_specs=[pl.BlockSpec(memory_space=pl.ANY)] * 3,
        out_specs=(pl.BlockSpec(memory_space=pltpu.VMEM), pl.BlockSpec(memory_space=pltpu.VMEM)),
        scratch_shapes=[
            pltpu.VMEM((64, 1024), BF),
            pltpu.VMEM((8, OWN), jnp.int32),
            pltpu.VMEM((16, 32, 128), BF),
            pltpu.VMEM((16, 32, 128), BF),
            pltpu.VMEM((OWN, TILE, 512), BF),
            pltpu.VMEM((2, 3, 4, TILE, 512), BF),
            pltpu.VMEM((16, 128), jnp.int32),
            pltpu.VMEM((2, 16, 128), jnp.int32),
            pltpu.SMEM((3, 16, 128), jnp.int32),
            pltpu.VMEM((4, 9, TILE, 128), BF),
            pltpu.VMEM((10 * GROUP, WIN), BF),
            pltpu.VMEM((2, 16, 32, 128), BF),
            pltpu.VMEM((2, 16, 32, 128), BF),
            pltpu.VMEM((2, 8, 32, 128), BF),
            pltpu.VMEM((2, ext, 64), BF),
            pltpu.VMEM((2, ext, 64), F32),
            pltpu.VMEM((16, 32, 128), BF),
            pltpu.VMEM((8, 32, 128), BF),
            pltpu.VMEM((4, 4, 32, 128), BF),
            pltpu.VMEM((4, 4, 4, 32, 128), BF),
            pltpu.VMEM((8, 256, 128), BF),
            pltpu.VMEM((4, 256, 128), BF),
            pltpu.VMEM((4, 256, 128), BF),
            pltpu.VMEM((4, 256, 128), F32),
            pltpu.VMEM((4, 256, 128), BF),
            pltpu.VMEM((4, 256, 128), BF),
            pltpu.VMEM((256, 128), BF),
            pltpu.VMEM((8, 64, 128), BF),
            pltpu.VMEM((8, 64, 128), BF),
            pltpu.SemaphoreType.DMA((4,)),
            pltpu.SemaphoreType.DMA((COUNT,)),
            pltpu.SemaphoreType.DMA((COUNT,)),
        ],
        compiler_params=pltpu.CompilerParams(
            collective_id=0, has_side_effects=True, vmem_limit_bytes=48 * 1024 * 1024
        ),
        name="filter_and_gram",
    )(*(pltpu.with_memory_space_constraint(v, pltpu.HBM) for v in (search_vectors, block_columns.T, tile_values)))


def solution(mesh):
    return jax.shard_map(
        per_device,
        mesh=mesh,
        in_specs=(P(("rows", "cols"), None), P("rows", None, None), P("rows", None)),
        out_specs=(P(("rows", "cols"), None), P("cols", None)),
        check_vma=False,
    )
```

```python
import jax
import jax.numpy as jnp
from jax import lax
from jax.experimental import pallas as pl
from jax.experimental.pallas import tpu as pltpu
from jax.sharding import PartitionSpec as P

MESH = pl.DeviceIdType.MESH
BF, F32 = jnp.bfloat16, jnp.float32

TILE = 64
OWN = 16
GROUP = 256
WIN = 768
SCALE = 1.0 / 16384

A2A, TIL, IDX, VEC, EARLY, OLD, LATE = 0, 16, 22, 24, 26, 28, 30
QUART, GATH, PAIR, XRED, ZRED, SPREAD, RELAY, COUNT = 32, 36, 52, 56, 72, 80, 88, 96


def swap(v):
    return jnp.concatenate([v[:, 64:], v[:, :64]], axis=1)


def pack(block):
    return jnp.concatenate([block[:32], block[32:]], axis=1)


def kernel(
    x_hbm, cols_hbm, tiles_hbm, out_ref, gram_ref,
    x_ref, cols_ref, xs, xr, tv, th, idxv, idxh, idxs, slab, band, hx, hp, ho, w0, w1, y0, y1,
    fp, op, fq, pc, fy, gs, gr, gf, xsnd, xrcv, zs, zr, ro, local_sem, ss, rs,
):
    r, c = lax.axis_index("rows"), lax.axis_index("cols")
    yy, zh = lax.rem(c, 4), c // 4
    core, x, zl = lax.rem(r, 2), lax.rem(r // 2, 4), r // 8
    z = zh * 2 + zl
    w, y = (w0, w1), (y0, y1)

    def remote(src, dst, number, device):
        return pltpu.make_async_remote_copy(
            src_ref=src, dst_ref=dst, send_sem=ss.at[number], recv_sem=rs.at[number],
            device_id=device, device_id_type=MESH,
        )

    own_x = pltpu.make_async_copy(x_hbm, x_ref, local_sem.at[0])
    own_cols = pltpu.make_async_copy(cols_hbm, cols_ref, local_sem.at[1])
    own_tiles = pltpu.make_async_copy(tiles_hbm, tv, local_sem.at[2])

    barrier = pltpu.get_barrier_semaphore()

    def greet(device):
        pl.semaphore_signal(barrier, inc=1, device_id=device, device_id_type=MESH)

    for i in (8, 7, 9, 6, 10, 5, 11, 4, 12, 3, 13, 2, 14, 1, 15):
        greet((r, lax.rem(c + i, 16)))
    for i in range(4):
        greet((lax.rem(r + 8, 16), lax.rem(zh + i, 4) * 4 + yy))
    for i in range(1, 8):
        greet((zl * 8 + lax.rem(r + i, 8), c))
    at_7, at_8 = r == 7, r == 8
    middle = jnp.logical_or(at_7, at_8)
    turned = jnp.where(at_7, lax.rem(zh + 3, 4), lax.rem(zh + 1, 4)) * 4 + yy
    @pl.when(middle)
    def _():
        greet((15 - r, c))
        greet((15 - r, turned))

    own_x.start()
    own_cols.start()
    own_tiles.start()

    has_low, has_high = r > 0, r < 15
    edges = (has_low, has_high)
    up, down = jnp.minimum(r + 1, 15), jnp.maximum(r - 1, 0)

    def zero(ref, first, count):
        ref[pl.ds(first, count), :] = jnp.zeros((count, ref.shape[1]), ref.dtype)

    for side in range(2):

        @pl.when(jnp.logical_not(edges[side]))
        def _(side=side):
            zero(band, 7 * side * GROUP, 3 * GROUP)
            zero(w[0], side * 8 * GROUP, 4 * GROUP)

    for u in range(4):
        slab[u, 8] = jnp.zeros((TILE, 128), BF)

    own_x.wait()
    for g in range(16):
        xs[g] = pack(x_ref[:, g * 64 : (g + 1) * 64])

    own_cols.wait()
    slot = lax.broadcasted_iota(jnp.int32, (16, OWN), 0)
    first_col = r * OWN + (lax.broadcasted_iota(jnp.int32, (8, OWN), 1) // 4) * 4 - 4
    places = cols_ref[...] - first_col
    slabs = jnp.full((16, OWN), 8, jnp.int32)
    for k in range(8):
        which = jnp.where(lax.rem(slot, 2) == 0, k, k + 1 - 2 * (k % 2))
        slabs = jnp.where(slot == places[k : k + 1, :], which, slabs)
    idxv[...] = jnp.zeros_like(idxv)
    idxv[:, :OWN] = slabs

    pl.when(middle)(lambda: pl.semaphore_wait(barrier, 28))
    pl.when(jnp.logical_not(middle))(lambda: pl.semaphore_wait(barrier, 26))

    a2a = []
    for i in (8, 7, 9, 6, 10, 5, 11, 4, 12, 3, 13, 2, 14, 1, 15):
        to = lax.rem(c + i, 16)
        copy = remote(xs.at[to], xr.at[c], A2A + i, (r, to))
        copy.start()
        a2a.append(copy)

    def both_sides(number, to_up, to_down, low_dst, high_dst, col_up=c, col_down=c):
        a = remote(to_up, low_dst, number, (up, col_up))
        b = remote(to_down, high_dst, number + 1, (down, col_down))
        pl.when(has_high)(a.start)
        pl.when(has_low)(b.start)
        return a, b

    def arrived(pair):
        pl.when(has_low)(pair[0].wait_recv)
        pl.when(has_high)(pair[1].wait_recv)

    def sent(pair):
        pl.when(has_high)(pair[0].wait_send)
        pl.when(has_low)(pair[1].wait_send)

    idx = both_sides(IDX, idxv, idxv, idxh.at[0], idxh.at[1])
    mine_of = [th.at[side, 2, pl.ds(yy, 1)] for side in range(2)]
    far = both_sides(
        TIL + 4, tiles_hbm.at[pl.ds(4 + yy, 1)], tiles_hbm.at[pl.ds(8 + yy, 1)], *mine_of
    )
    til = [
        both_sides(
            TIL + 2 * n, tiles_hbm.at[pl.ds(4 * (3 - n), 4)], tiles_hbm.at[pl.ds(4 * n, 4)],
            th.at[0, n], th.at[1, n],
            *((jnp.where(at_7, turned, c), jnp.where(at_8, turned, c)) if n == 1 else (c, c)),
        )
        for n in range(2)
    ]
    relay = [
        [
            remote(v, v, RELAY + 4 * side + j, (r, zh * 4 + lax.rem(yy + j, 4)))
            for j in (2, 1, 3)
        ]
        for side, v in enumerate(mine_of)
    ]

    def on_side(side, method):
        @pl.when(edges[side])
        def _():
            for copy in relay[side]:
                getattr(copy, method)()

    xr[c] = xs[c]

    low_lanes = lax.broadcasted_iota(jnp.int32, (TILE, 128), 1) < 64

    def place(tiles, source, first, at):
        for u in range(4):
            for p in range(4):
                piece = tiles[u, :, p * 128 : (p + 1) * 128]
                slab[u, 2 * p] = piece
                slab[u, 2 * p + 1] = swap(piece)
            for j in range(6):
                left = slab[u, idxs[source, 2 * j, first + u]]
                right = slab[u, idxs[source, 2 * j + 1, first + u]]
                band[pl.ds(at + u * TILE, TILE), j * 128 : (j + 1) * 128] = jnp.where(
                    low_lanes, left, right
                )

    def to_smem(src, number):
        copy = pltpu.make_async_copy(src, idxs.at[number], local_sem.at[3])
        copy.start()
        copy.wait()

    to_smem(idxv, 2)
    own_tiles.wait()

    def place_own(i, carry):
        at = pl.multiple_of((3 + i) * GROUP, GROUP)
        place(tv.at[pl.ds(4 * i, 4)], 2, 4 * i, at)
        return carry

    lax.fori_loop(0, 4, place_own, 0)
    arrived(far)
    for side in range(2):
        on_side(side, "start")

    def unpack(v, block, ref):
        for half in range(2):
            rows = pl.ds(block * TILE + half * 32, 32)
            ref[rows, :] = v[:, half * 64 : (half + 1) * 64].astype(ref.dtype)

    def one(n, k, turn=False):
        g = jnp.where(core == 0, k, 11 - k) if turn else k
        now, later = n % 2, (n + 1) % 2
        at = g * GROUP if isinstance(g, int) else pl.multiple_of(g * GROUP, GROUP)
        back = (g - 1) * GROUP if isinstance(g, int) else pl.multiple_of((g - 1) * GROUP, GROUP)
        rows = pl.ds(at, GROUP)
        product = jnp.dot(
            band[pl.ds(back, GROUP), :], w[now][pl.ds(back, WIN), :], preferred_element_type=F32
        )
        outer = n in (4, 5) and not 4 <= k <= 7
        current = w[now][rows, :].astype(F32) if n == 0 or (n == 4 and outer) else y[now][rows, :]
        if n == 0:
            new = (product - 0.1 * current) * 0.5
        else:
            before = w if n == 1 or (n == 5 and outer) else y
            new = product - 0.1 * current - before[later][rows, :].astype(F32)
        rounded = new.astype(BF)
        if n < 7:
            y[later][rows, :] = new
            w[later][rows, :] = rounded
        return rounded

    for copy in a2a:
        copy.wait_recv()
    vec = both_sides(VEC, xr, xr, hx.at[0], hx.at[1])
    for b in range(OWN):
        unpack(xr[b], OWN + b, w[0])
    for g in (5, 6):
        one(0, g)

    arrived(idx)
    for side in range(2):

        @pl.when(edges[side])
        def _(side=side):
            to_smem(idxh.at[side], side)

    def on_fast(fast, work):
        for side in range(2):
            here = core == (1 - side if fast else side)
            pl.when(jnp.logical_and(here, edges[side]))(lambda side=side: work(side))

    def place_chunk(side, n):
        place(
            th.at[side, n], side, 4 * (3 - n) if side == 0 else 4 * n,
            (2 - n if side == 0 else 7 + n) * GROUP,
        )

    def near_chunks(side):
        for n in range(2):
            til[n][side].wait_recv()
            place_chunk(side, n)

    def vectors(side):
        vec[side].wait_recv()
        for b in range(OWN):
            unpack(hx[side, b], side * 2 * OWN + b, w[0])

    def far_chunk(side):
        for copy in relay[side]:
            copy.wait_recv()
        place_chunk(side, 2)

    on_fast(True, near_chunks)
    on_fast(True, vectors)
    for n, k in ((0, 7), (0, 8), (0, 9), (1, 6), (1, 7), (1, 8), (2, 7)):
        one(n, k, True)
    on_fast(False, near_chunks)
    on_fast(False, vectors)
    for n, k in ((0, 4), (0, 3), (0, 2), (1, 5), (1, 4), (1, 3), (2, 6), (2, 5), (2, 4)):
        one(n, k, True)

    for b in range(8):
        op[b] = pack(y[1][pl.ds((20 + b) * TILE, TILE), :]).astype(BF)
    old = both_sides(OLD, op, op, ho.at[0], ho.at[1])

    def pack_group(rounded, dst, first):
        for b in range(4):
            dst[first + b] = pack(rounded[b * TILE : (b + 1) * TILE])

    for slot, g in ((0, 5), (4, 6)):
        pack_group(one(3, g), fp, slot)
    early = both_sides(
        EARLY, fp.at[pl.ds(0, 8)], fp.at[pl.ds(0, 8)], hp.at[0, pl.ds(0, 8)], hp.at[1, pl.ds(0, 8)]
    )
    on_fast(True, far_chunk)
    on_fast(False, far_chunk)
    for n, g in ((0, 1), (0, 10), (1, 2), (1, 9), (2, 3), (2, 8)):
        one(n, g)
    for slot, g in ((8, 4), (12, 7)):
        pack_group(one(3, g), fp, slot)
    late = both_sides(
        LATE, fp.at[pl.ds(8, 8)], fp.at[pl.ds(8, 8)], hp.at[0, pl.ds(8, 8)], hp.at[1, pl.ds(8, 8)]
    )
    for g in (5, 6):
        one(4, g)

    def later_vectors(side):
        for pair in (old, early, late):
            pair[side].wait_recv()
        first = side * 2 * OWN
        for b in range(8):
            unpack(hp[side, b], first + 4 + b, w[0])
            unpack(ho[side, b], first + 4 + b, y[1])
            unpack(hp[side, 8 + b], first + (b if b < 4 else b + 8), w[0])

    on_fast(True, later_vectors)
    for n, ks in ((4, (7, 8, 9, 10)), (5, (6, 7, 8, 9)), (6, (7, 8))):
        for k in ks:
            one(n, k, True)
    on_fast(False, later_vectors)
    for n, ks in ((4, (4, 3, 2, 1)), (5, (5, 4, 3, 2)), (6, (6, 5, 4, 3))):
        for k in ks:
            one(n, k, True)

    quart, gath = [], {}
    for i in (2, 1, 3, 0):
        to = lax.rem(zh + i, 4)
        rounded = one(7, 4 + to)
        if i:
            pack_group(rounded, fq.at[to], 0)
            copy = remote(fq.at[to], pc.at[yy, zh], QUART + i, (r, to * 4 + yy))
            copy.start()
            quart.append((i, copy))
        else:
            pack_group(rounded, pc.at[yy, zh], 0)

    def to_y(i):
        piece = pc.at[yy, lax.rem(zh - i + 4, 4)]
        for j in (2, 1, 3):
            device = (r, zh * 4 + lax.rem(yy + j, 4))
            copy = remote(piece, piece, GATH + 4 * i + j, device)
            copy.start()
            gath[i, j] = copy

    to_y(0)
    for i, copy in (quart[1], quart[2], quart[0]):
        copy.wait_recv()
        to_y(i)

    def assemble(who):
        for half in range(2):
            for b in range(4):
                left, right = pc[who, 2 * half, b], pc[who, 2 * half + 1, b]
                for part in range(2):
                    lanes = slice(part * 64, (part + 1) * 64)
                    fy[2 * who + half, pl.ds(b * TILE + part * 32, 32), :] = jnp.concatenate(
                        [left[:, lanes], right[:, lanes]], axis=1
                    )

    assemble(yy)
    mine = jnp.concatenate(
        [fy[2 * yy + half].astype(F32).T.astype(BF) for half in range(2)], axis=0
    )
    for j in (1, 3, 2):
        for i in range(4):
            gath[i, j].wait_recv()
        assemble(lax.rem(yy - j + 4, 4))

    pair_dev = (r + 1 - 2 * core, c)
    order = (2, 1, 3, 0)
    pairs = {}
    for i in order:
        to = lax.rem(x + i, 4)
        gs[i] = jnp.dot(mine, fy[(1 - core) * 4 + to], preferred_element_type=F32).astype(BF)
        pairs[i] = remote(gs.at[i], gr.at[i], PAIR + i, pair_dev)
        pairs[i].start()
    for i in order:
        gf[i] = jnp.dot(mine, fy[core * 4 + lax.rem(x + i, 4)], preferred_element_type=F32)

    xred = {}
    parts = [lax.rem(zh + d, 4) for d in (2, 1, 3, 0)]
    for i in order:
        pairs[i].wait_recv()
        total = gf[i] + gr[i].astype(F32)
        if i:
            xsnd[i] = total.astype(BF)
        else:
            gf[0] = total
    for k, part in enumerate(parts):
        rows = pl.ds(pl.multiple_of(part * 64, 64), 64)
        for i in order[:3]:
            device = (zl * 8 + lax.rem(x + i, 4) * 2 + core, c)
            xred[i, k] = remote(xsnd.at[i, rows], xrcv.at[i, rows], XRED + 4 * i + k, device)
            xred[i, k].start()

    rows = pl.ds(pl.multiple_of(yy * TILE, TILE), TILE)
    for h in range(4):
        for p in range(2):
            lanes = slice((h % 2) * 64, (h % 2 + 1) * 64)
            out_ref[:, h * 256 + p * 128 : h * 256 + (p + 1) * 128] = jnp.concatenate(
                [fy[4 * p + h // 2, rows, lanes], fy[4 * p + 2 + h // 2, rows, lanes]], axis=1
            )

    for k, part in enumerate(parts):
        rows = pl.ds(pl.multiple_of(part * 64, 64), 64)
        total = gf[0, rows, :]
        for i in order[:3]:
            xred[i, k].wait_recv()
            total = total + xrcv[i, rows, :].astype(F32)
        zs[rows, :] = total.astype(BF)
        for lo in (zl, 1 - zl) if k < 3 else (1 - zl,):
            i = lax.rem(part * 2 + lo - z + 8, 8)
            copy = remote(zs.at[rows], zr.at[z], ZRED + i, (lo * 8 + x * 2 + core, part * 4 + yy))
            copy.start()
    zr[z] = zs[pl.ds(pl.multiple_of(zh * 64, 64), 64), :]
    landed = [remote(zs.at[pl.ds(0, 64)], zr.at[z], ZRED + i, pair_dev) for i in range(1, 8)]
    for copy in landed:
        copy.wait_recv()
    total = zr[0].astype(F32)
    for i in range(1, 8):
        total = total + zr[i].astype(F32)
    rr = lax.rem(r, 8)
    ro[rr] = (total * SCALE).astype(BF)

    spread = []
    for i in (4, 3, 5, 2, 6, 7, 1):
        copy = remote(ro.at[rr], ro.at[rr], SPREAD + i, (zl * 8 + lax.rem(rr + i, 8), c))
        copy.start()
        spread.append(copy)

    for side in range(2):
        on_side(side, "wait_send")
    for pair in (idx, far, *til, vec, old, early, late):
        sent(pair)
    for copy in a2a + list(gath.values()):
        copy.wait_send()
    for i, copy in quart + list(pairs.items()):
        copy.wait_send()
    for copy in list(xred.values()) + landed:
        copy.wait_send()
    for copy in spread:
        copy.wait_recv()
    for h in range(4):
        for p in range(2):
            lanes = slice((h % 2) * 64, (h % 2 + 1) * 64)
            at = [(k * 2 + h // 2) * 2 + p for k in range(2)]
            gram_ref[:, h * 256 + p * 128 : h * 256 + (p + 1) * 128] = jnp.concatenate(
                [ro[at[0]][:, lanes], ro[at[1]][:, lanes]], axis=1
            ).astype(F32)
    for copy in spread:
        copy.wait_send()


def per_device(search_vectors, tile_values, block_columns):
    ext = 12 * GROUP
    return pl.pallas_call(
        kernel,
        out_shape=(
            jax.ShapeDtypeStruct((64, 1024), BF),
            jax.ShapeDtypeStruct((64, 1024), F32),
        ),
        in_specs=[pl.BlockSpec(memory_space=pl.ANY)] * 3,
        out_specs=(pl.BlockSpec(memory_space=pltpu.VMEM), pl.BlockSpec(memory_space=pltpu.VMEM)),
        scratch_shapes=[
            pltpu.VMEM((64, 1024), BF),
            pltpu.VMEM((8, OWN), jnp.int32),
            pltpu.VMEM((16, 32, 128), BF),
            pltpu.VMEM((16, 32, 128), BF),
            pltpu.VMEM((OWN, TILE, 512), BF),
            pltpu.VMEM((2, 3, 4, TILE, 512), BF),
            pltpu.VMEM((16, 128), jnp.int32),
            pltpu.VMEM((2, 16, 128), jnp.int32),
            pltpu.SMEM((3, 16, 128), jnp.int32),
            pltpu.VMEM((4, 9, TILE, 128), BF),
            pltpu.VMEM((10 * GROUP, WIN), BF),
            pltpu.VMEM((2, 16, 32, 128), BF),
            pltpu.VMEM((2, 16, 32, 128), BF),
            pltpu.VMEM((2, 8, 32, 128), BF),
            pltpu.VMEM((ext, 64), BF),
            pltpu.VMEM((ext, 64), BF),
            pltpu.VMEM((ext, 64), F32),
            pltpu.VMEM((ext, 64), F32),
            pltpu.VMEM((16, 32, 128), BF),
            pltpu.VMEM((8, 32, 128), BF),
            pltpu.VMEM((4, 4, 32, 128), BF),
            pltpu.VMEM((4, 4, 4, 32, 128), BF),
            pltpu.VMEM((8, 256, 128), BF),
            pltpu.VMEM((4, 256, 128), BF),
            pltpu.VMEM((4, 256, 128), BF),
            pltpu.VMEM((4, 256, 128), F32),
            pltpu.VMEM((4, 256, 128), BF),
            pltpu.VMEM((4, 256, 128), BF),
            pltpu.VMEM((256, 128), BF),
            pltpu.VMEM((8, 64, 128), BF),
            pltpu.VMEM((8, 64, 128), BF),
            pltpu.SemaphoreType.DMA((4,)),
            pltpu.SemaphoreType.DMA((COUNT,)),
            pltpu.SemaphoreType.DMA((COUNT,)),
        ],
        compiler_params=pltpu.CompilerParams(
            collective_id=0, has_side_effects=True, vmem_limit_bytes=48 * 1024 * 1024
        ),
        name="filter_and_gram",
    )(*(pltpu.with_memory_space_constraint(v, pltpu.HBM) for v in (search_vectors, block_columns.T, tile_values)))


def solution(mesh):
    return jax.shard_map(
        per_device,
        mesh=mesh,
        in_specs=(P(("rows", "cols"), None), P("rows", None, None), P("rows", None)),
        out_specs=(P(("rows", "cols"), None), P("cols", None)),
        check_vma=False,
    )
```

```python
import jax
import jax.numpy as jnp
from jax import lax
from jax.experimental import pallas as pl
from jax.experimental.pallas import tpu as pltpu
from jax.sharding import PartitionSpec as P

MESH = pl.DeviceIdType.MESH
BF, F32 = jnp.bfloat16, jnp.float32

TILE = 64
OWN = 16
GROUP = 256
WIN = 768
SCALE = 1.0 / 16384

A2A, TIL, IDX, VEC, EARLY, OLD, LATE = 0, 16, 22, 24, 26, 28, 30
QUART, GATH, PAIR, XRED, ZRED, SPREAD, RELAY, COUNT = 32, 36, 52, 56, 72, 80, 88, 96


def swap(v):
    return jnp.concatenate([v[:, 64:], v[:, :64]], axis=1)


def pack(block):
    return jnp.concatenate([block[:32], block[32:]], axis=1)


def kernel(
    x_hbm, cols_hbm, tiles_hbm, out_ref, gram_ref,
    x_ref, cols_ref, xs, xr, tv, th, idxv, idxh, idxs, slab, band, hx, hp, ho, w0, w1, y0, y1,
    fp, op, fq, pc, fy, gs, gr, gf, xsnd, xrcv, zs, zr, ro, local_sem, ss, rs,
):
    r, c = lax.axis_index("rows"), lax.axis_index("cols")
    yy, zh = lax.rem(c, 4), c // 4
    core, x, zl = lax.rem(r, 2), lax.rem(r // 2, 4), r // 8
    z = zh * 2 + zl
    w, y = (w0, w1), (y0, y1)

    def remote(src, dst, number, device):
        return pltpu.make_async_remote_copy(
            src_ref=src, dst_ref=dst, send_sem=ss.at[number], recv_sem=rs.at[number],
            device_id=device, device_id_type=MESH,
        )

    own_x = pltpu.make_async_copy(x_hbm, x_ref, local_sem.at[0])
    own_cols = pltpu.make_async_copy(cols_hbm, cols_ref, local_sem.at[1])
    own_tiles = pltpu.make_async_copy(tiles_hbm, tv, local_sem.at[2])

    barrier = pltpu.get_barrier_semaphore()

    def greet(device):
        pl.semaphore_signal(barrier, inc=1, device_id=device, device_id_type=MESH)

    for i in (8, 7, 9, 6, 10, 5, 11, 4, 12, 3, 13, 2, 14, 1, 15):
        greet((r, lax.rem(c + i, 16)))
    for i in range(4):
        greet((lax.rem(r + 8, 16), lax.rem(zh + i, 4) * 4 + yy))
    for i in range(1, 8):
        greet((zl * 8 + lax.rem(r + i, 8), c))
    at_7, at_8 = r == 7, r == 8
    middle = jnp.logical_or(at_7, at_8)
    turned = jnp.where(at_7, lax.rem(zh + 3, 4), lax.rem(zh + 1, 4)) * 4 + yy
    @pl.when(middle)
    def _():
        greet((15 - r, c))
        greet((15 - r, turned))

    own_x.start()
    own_cols.start()
    own_tiles.start()

    has_low, has_high = r > 0, r < 15
    edges = (has_low, has_high)
    up, down = jnp.minimum(r + 1, 15), jnp.maximum(r - 1, 0)

    def zero(ref, first, count):
        ref[pl.ds(first, count), :] = jnp.zeros((count, ref.shape[1]), ref.dtype)

    for side in range(2):

        @pl.when(jnp.logical_not(edges[side]))
        def _(side=side):
            zero(band, 7 * side * GROUP, 3 * GROUP)
            zero(w[0], side * 8 * GROUP, 4 * GROUP)

    for u in range(4):
        slab[u, 8] = jnp.zeros((TILE, 128), BF)

    own_x.wait()
    for g in range(16):
        xs[g] = pack(x_ref[:, g * 64 : (g + 1) * 64])

    own_cols.wait()
    slot = lax.broadcasted_iota(jnp.int32, (16, OWN), 0)
    first_col = r * OWN + (lax.broadcasted_iota(jnp.int32, (8, OWN), 1) // 4) * 4 - 4
    places = cols_ref[...] - first_col
    slabs = jnp.full((16, OWN), 8, jnp.int32)
    for k in range(8):
        which = jnp.where(lax.rem(slot, 2) == 0, k, k + 1 - 2 * (k % 2))
        slabs = jnp.where(slot == places[k : k + 1, :], which, slabs)
    idxv[...] = jnp.zeros_like(idxv)
    idxv[:, :OWN] = slabs

    pl.when(middle)(lambda: pl.semaphore_wait(barrier, 28))
    pl.when(jnp.logical_not(middle))(lambda: pl.semaphore_wait(barrier, 26))

    a2a = []
    for i in (8, 7, 9, 6, 10, 5, 11, 4, 12, 3, 13, 2, 14, 1, 15):
        to = lax.rem(c + i, 16)
        copy = remote(xs.at[to], xr.at[c], A2A + i, (r, to))
        copy.start()
        a2a.append(copy)

    def both_sides(number, to_up, to_down, low_dst, high_dst, col_up=c, col_down=c):
        a = remote(to_up, low_dst, number, (up, col_up))
        b = remote(to_down, high_dst, number + 1, (down, col_down))
        pl.when(has_high)(a.start)
        pl.when(has_low)(b.start)
        return a, b

    def arrived(pair):
        pl.when(has_low)(pair[0].wait_recv)
        pl.when(has_high)(pair[1].wait_recv)

    def sent(pair):
        pl.when(has_high)(pair[0].wait_send)
        pl.when(has_low)(pair[1].wait_send)

    idx = both_sides(IDX, idxv, idxv, idxh.at[0], idxh.at[1])
    def on_fast(fast, work):
        for side in range(2):
            here = core == (1 - side if fast else side)
            pl.when(jnp.logical_and(here, edges[side]))(lambda side=side: work(side))

    mine_of = [th.at[side, 2, pl.ds(yy, 1)] for side in range(2)]
    whole = (
        remote(tiles_hbm.at[pl.ds(4, 4)], th.at[0, 2], TIL + 4, (up, c)),
        remote(tiles_hbm.at[pl.ds(8, 4)], th.at[1, 2], TIL + 5, (down, c)),
    )
    shared = (
        remote(tiles_hbm.at[pl.ds(4 + yy, 1)], mine_of[0], TIL + 4, (up, c)),
        remote(tiles_hbm.at[pl.ds(8 + yy, 1)], mine_of[1], TIL + 5, (down, c)),
    )

    def far_out(method):
        pl.when(jnp.logical_and(core == 1, has_high))(lambda: getattr(shared[0], method)())
        pl.when(jnp.logical_and(core == 0, has_low))(lambda: getattr(shared[1], method)())
        pl.when(core == 0)(lambda: getattr(whole[0], method)())
        pl.when(core == 1)(lambda: getattr(whole[1], method)())

    far_out("start")
    til = [
        both_sides(
            TIL + 2 * n, tiles_hbm.at[pl.ds(4 * (3 - n), 4)], tiles_hbm.at[pl.ds(4 * n, 4)],
            th.at[0, n], th.at[1, n],
            *((jnp.where(at_7, turned, c), jnp.where(at_8, turned, c)) if n == 1 else (c, c)),
        )
        for n in range(2)
    ]
    relay = [
        [
            remote(v, v, RELAY + 4 * side + j, (r, zh * 4 + lax.rem(yy + j, 4)))
            for j in (2, 1, 3)
        ]
        for side, v in enumerate(mine_of)
    ]

    xr[c] = xs[c]

    low_lanes = lax.broadcasted_iota(jnp.int32, (TILE, 128), 1) < 64

    def place(tiles, source, first, at):
        for u in range(4):
            for p in range(4):
                piece = tiles[u, :, p * 128 : (p + 1) * 128]
                slab[u, 2 * p] = piece
                slab[u, 2 * p + 1] = swap(piece)
            for j in range(6):
                left = slab[u, idxs[source, 2 * j, first + u]]
                right = slab[u, idxs[source, 2 * j + 1, first + u]]
                band[pl.ds(at + u * TILE, TILE), j * 128 : (j + 1) * 128] = jnp.where(
                    low_lanes, left, right
                )

    def to_smem(src, number):
        copy = pltpu.make_async_copy(src, idxs.at[number], local_sem.at[3])
        copy.start()
        copy.wait()

    to_smem(idxv, 2)
    own_tiles.wait()

    def place_own(i, carry):
        at = pl.multiple_of((3 + i) * GROUP, GROUP)
        place(tv.at[pl.ds(4 * i, 4)], 2, 4 * i, at)
        return carry

    lax.fori_loop(0, 4, place_own, 0)

    def pass_on(side):
        shared[side].wait_recv()
        for copy in relay[side]:
            copy.start()

    on_fast(False, pass_on)

    def unpack(v, block, ref):
        for half in range(2):
            rows = pl.ds(block * TILE + half * 32, 32)
            ref[rows, :] = v[:, half * 64 : (half + 1) * 64].astype(ref.dtype)

    def one(n, k, turn=False):
        g = jnp.where(core == 0, k, 11 - k) if turn else k
        now, later = n % 2, (n + 1) % 2
        at = g * GROUP if isinstance(g, int) else pl.multiple_of(g * GROUP, GROUP)
        back = (g - 1) * GROUP if isinstance(g, int) else pl.multiple_of((g - 1) * GROUP, GROUP)
        rows = pl.ds(at, GROUP)
        product = jnp.dot(
            band[pl.ds(back, GROUP), :], w[now][pl.ds(back, WIN), :], preferred_element_type=F32
        )
        outer = n in (4, 5) and not 4 <= k <= 7
        current = w[now][rows, :].astype(F32) if n == 0 or (n == 4 and outer) else y[now][rows, :]
        if n == 0:
            new = (product - 0.1 * current) * 0.5
        else:
            before = w if n == 1 or (n == 5 and outer) else y
            new = product - 0.1 * current - before[later][rows, :].astype(F32)
        rounded = new.astype(BF)
        if n < 7:
            y[later][rows, :] = new
            w[later][rows, :] = rounded
        return rounded

    for copy in a2a:
        copy.wait_recv()
    vec = both_sides(VEC, xr, xr, hx.at[0], hx.at[1])
    for b in range(OWN):
        unpack(xr[b], OWN + b, w[0])
    for g in (5, 6):
        one(0, g)

    arrived(idx)
    for side in range(2):

        @pl.when(edges[side])
        def _(side=side):
            to_smem(idxh.at[side], side)

    def place_chunk(side, n):
        place(
            th.at[side, n], side, 4 * (3 - n) if side == 0 else 4 * n,
            (2 - n if side == 0 else 7 + n) * GROUP,
        )

    def near_chunks(side):
        for n in range(2):
            til[n][side].wait_recv()
            place_chunk(side, n)

    def vectors(side):
        vec[side].wait_recv()
        for b in range(OWN):
            unpack(hx[side, b], side * 2 * OWN + b, w[0])

    def far_chunk_here(side):
        whole[side].wait_recv()
        place_chunk(side, 2)

    def far_chunk(side):
        for copy in relay[side]:
            copy.wait_recv()
        place_chunk(side, 2)

    on_fast(True, near_chunks)
    on_fast(True, far_chunk_here)
    on_fast(True, vectors)
    for n, k in ((0, 7), (0, 8), (0, 9), (1, 6), (1, 7), (1, 8), (2, 7)):
        one(n, k, True)
    on_fast(False, near_chunks)
    on_fast(False, vectors)
    for n, k in ((0, 4), (0, 3), (0, 2), (1, 5), (1, 4), (1, 3), (2, 6), (2, 5), (2, 4)):
        one(n, k, True)

    for b in range(8):
        op[b] = pack(y[1][pl.ds((20 + b) * TILE, TILE), :]).astype(BF)
    old = both_sides(OLD, op, op, ho.at[0], ho.at[1])

    def pack_group(rounded, dst, first):
        for b in range(4):
            dst[first + b] = pack(rounded[b * TILE : (b + 1) * TILE])

    for slot, g in ((0, 5), (4, 6)):
        pack_group(one(3, g), fp, slot)
    early = both_sides(
        EARLY, fp.at[pl.ds(0, 8)], fp.at[pl.ds(0, 8)], hp.at[0, pl.ds(0, 8)], hp.at[1, pl.ds(0, 8)]
    )
    on_fast(False, far_chunk)
    for n, g in ((0, 1), (0, 10), (1, 2), (1, 9), (2, 3), (2, 8)):
        one(n, g)
    for slot, g in ((8, 4), (12, 7)):
        pack_group(one(3, g), fp, slot)
    late = both_sides(
        LATE, fp.at[pl.ds(8, 8)], fp.at[pl.ds(8, 8)], hp.at[0, pl.ds(8, 8)], hp.at[1, pl.ds(8, 8)]
    )
    for g in (5, 6):
        one(4, g)

    def later_vectors(side):
        for pair in (old, early, late):
            pair[side].wait_recv()
        first = side * 2 * OWN
        for b in range(8):
            unpack(hp[side, b], first + 4 + b, w[0])
            unpack(ho[side, b], first + 4 + b, y[1])
            unpack(hp[side, 8 + b], first + (b if b < 4 else b + 8), w[0])

    on_fast(True, later_vectors)
    for n, ks in ((4, (7, 8, 9, 10)), (5, (6, 7, 8, 9)), (6, (7, 8))):
        for k in ks:
            one(n, k, True)
    on_fast(False, later_vectors)
    for n, ks in ((4, (4, 3, 2, 1)), (5, (5, 4, 3, 2)), (6, (6, 5, 4, 3))):
        for k in ks:
            one(n, k, True)

    quart, gath = [], {}
    for i in (2, 1, 3, 0):
        to = lax.rem(zh + i, 4)
        rounded = one(7, 4 + to)
        if i:
            pack_group(rounded, fq.at[to], 0)
            copy = remote(fq.at[to], pc.at[yy, zh], QUART + i, (r, to * 4 + yy))
            copy.start()
            quart.append((i, copy))
        else:
            pack_group(rounded, pc.at[yy, zh], 0)

    def to_y(i):
        piece = pc.at[yy, lax.rem(zh - i + 4, 4)]
        for j in (2, 1, 3):
            device = (r, zh * 4 + lax.rem(yy + j, 4))
            copy = remote(piece, piece, GATH + 4 * i + j, device)
            copy.start()
            gath[i, j] = copy

    to_y(0)
    for i, copy in (quart[1], quart[2], quart[0]):
        copy.wait_recv()
        to_y(i)

    def assemble(who):
        for half in range(2):
            for b in range(4):
                left, right = pc[who, 2 * half, b], pc[who, 2 * half + 1, b]
                for part in range(2):
                    lanes = slice(part * 64, (part + 1) * 64)
                    fy[2 * who + half, pl.ds(b * TILE + part * 32, 32), :] = jnp.concatenate(
                        [left[:, lanes], right[:, lanes]], axis=1
                    )

    assemble(yy)
    mine = jnp.concatenate(
        [fy[2 * yy + half].astype(F32).T.astype(BF) for half in range(2)], axis=0
    )
    for j in (1, 3, 2):
        for i in range(4):
            gath[i, j].wait_recv()
        assemble(lax.rem(yy - j + 4, 4))

    pair_dev = (r + 1 - 2 * core, c)
    order = (2, 1, 3, 0)
    pairs = {}
    for i in order:
        to = lax.rem(x + i, 4)
        gs[i] = jnp.dot(mine, fy[(1 - core) * 4 + to], preferred_element_type=F32).astype(BF)
        pairs[i] = remote(gs.at[i], gr.at[i], PAIR + i, pair_dev)
        pairs[i].start()
    for i in order:
        gf[i] = jnp.dot(mine, fy[core * 4 + lax.rem(x + i, 4)], preferred_element_type=F32)

    xred = {}
    parts = [lax.rem(zh + d, 4) for d in (2, 1, 3, 0)]
    for i in order:
        pairs[i].wait_recv()
        total = gf[i] + gr[i].astype(F32)
        if i:
            xsnd[i] = total.astype(BF)
        else:
            gf[0] = total
    for k, part in enumerate(parts):
        rows = pl.ds(pl.multiple_of(part * 64, 64), 64)
        for i in order[:3]:
            device = (zl * 8 + lax.rem(x + i, 4) * 2 + core, c)
            xred[i, k] = remote(xsnd.at[i, rows], xrcv.at[i, rows], XRED + 4 * i + k, device)
            xred[i, k].start()

    rows = pl.ds(pl.multiple_of(yy * TILE, TILE), TILE)
    for h in range(4):
        for p in range(2):
            lanes = slice((h % 2) * 64, (h % 2 + 1) * 64)
            out_ref[:, h * 256 + p * 128 : h * 256 + (p + 1) * 128] = jnp.concatenate(
                [fy[4 * p + h // 2, rows, lanes], fy[4 * p + 2 + h // 2, rows, lanes]], axis=1
            )

    for k, part in enumerate(parts):
        rows = pl.ds(pl.multiple_of(part * 64, 64), 64)
        total = gf[0, rows, :]
        for i in order[:3]:
            xred[i, k].wait_recv()
            total = total + xrcv[i, rows, :].astype(F32)
        zs[rows, :] = total.astype(BF)
        for lo in (zl, 1 - zl) if k < 3 else (1 - zl,):
            i = lax.rem(part * 2 + lo - z + 8, 8)
            copy = remote(zs.at[rows], zr.at[z], ZRED + i, (lo * 8 + x * 2 + core, part * 4 + yy))
            copy.start()
    zr[z] = zs[pl.ds(pl.multiple_of(zh * 64, 64), 64), :]
    landed = [remote(zs.at[pl.ds(0, 64)], zr.at[z], ZRED + i, pair_dev) for i in range(1, 8)]
    for copy in landed:
        copy.wait_recv()
    total = zr[0].astype(F32)
    for i in range(1, 8):
        total = total + zr[i].astype(F32)
    rr = lax.rem(r, 8)
    ro[rr] = (total * SCALE).astype(BF)

    spread = []
    for i in (4, 3, 5, 2, 6, 7, 1):
        copy = remote(ro.at[rr], ro.at[rr], SPREAD + i, (zl * 8 + lax.rem(rr + i, 8), c))
        copy.start()
        spread.append(copy)

    def passed_on(side):
        for copy in relay[side]:
            copy.wait_send()

    on_fast(False, passed_on)
    far_out("wait_send")
    for pair in (idx, *til, vec, old, early, late):
        sent(pair)
    for copy in a2a + list(gath.values()):
        copy.wait_send()
    for i, copy in quart + list(pairs.items()):
        copy.wait_send()
    for copy in list(xred.values()) + landed:
        copy.wait_send()
    for copy in spread:
        copy.wait_recv()
    for h in range(4):
        for p in range(2):
            lanes = slice((h % 2) * 64, (h % 2 + 1) * 64)
            at = [(k * 2 + h // 2) * 2 + p for k in range(2)]
            gram_ref[:, h * 256 + p * 128 : h * 256 + (p + 1) * 128] = jnp.concatenate(
                [ro[at[0]][:, lanes], ro[at[1]][:, lanes]], axis=1
            ).astype(F32)
    for copy in spread:
        copy.wait_send()


def per_device(search_vectors, tile_values, block_columns):
    ext = 12 * GROUP
    return pl.pallas_call(
        kernel,
        out_shape=(
            jax.ShapeDtypeStruct((64, 1024), BF),
            jax.ShapeDtypeStruct((64, 1024), F32),
        ),
        in_specs=[pl.BlockSpec(memory_space=pl.ANY)] * 3,
        out_specs=(pl.BlockSpec(memory_space=pltpu.VMEM), pl.BlockSpec(memory_space=pltpu.VMEM)),
        scratch_shapes=[
            pltpu.VMEM((64, 1024), BF),
            pltpu.VMEM((8, OWN), jnp.int32),
            pltpu.VMEM((16, 32, 128), BF),
            pltpu.VMEM((16, 32, 128), BF),
            pltpu.VMEM((OWN, TILE, 512), BF),
            pltpu.VMEM((2, 3, 4, TILE, 512), BF),
            pltpu.VMEM((16, 128), jnp.int32),
            pltpu.VMEM((2, 16, 128), jnp.int32),
            pltpu.SMEM((3, 16, 128), jnp.int32),
            pltpu.VMEM((4, 9, TILE, 128), BF),
            pltpu.VMEM((10 * GROUP, WIN), BF),
            pltpu.VMEM((2, 16, 32, 128), BF),
            pltpu.VMEM((2, 16, 32, 128), BF),
            pltpu.VMEM((2, 8, 32, 128), BF),
            pltpu.VMEM((ext, 64), BF),
            pltpu.VMEM((ext, 64), BF),
            pltpu.VMEM((ext, 64), F32),
            pltpu.VMEM((ext, 64), F32),
            pltpu.VMEM((16, 32, 128), BF),
            pltpu.VMEM((8, 32, 128), BF),
            pltpu.VMEM((4, 4, 32, 128), BF),
            pltpu.VMEM((4, 4, 4, 32, 128), BF),
            pltpu.VMEM((8, 256, 128), BF),
            pltpu.VMEM((4, 256, 128), BF),
            pltpu.VMEM((4, 256, 128), BF),
            pltpu.VMEM((4, 256, 128), F32),
            pltpu.VMEM((4, 256, 128), BF),
            pltpu.VMEM((4, 256, 128), BF),
            pltpu.VMEM((256, 128), BF),
            pltpu.VMEM((8, 64, 128), BF),
            pltpu.VMEM((8, 64, 128), BF),
            pltpu.SemaphoreType.DMA((4,)),
            pltpu.SemaphoreType.DMA((COUNT,)),
            pltpu.SemaphoreType.DMA((COUNT,)),
        ],
        compiler_params=pltpu.CompilerParams(
            collective_id=0, has_side_effects=True, vmem_limit_bytes=48 * 1024 * 1024
        ),
        name="filter_and_gram",
    )(*(pltpu.with_memory_space_constraint(v, pltpu.HBM) for v in (search_vectors, block_columns.T, tile_values)))


def solution(mesh):
    return jax.shard_map(
        per_device,
        mesh=mesh,
        in_specs=(P(("rows", "cols"), None), P("rows", None, None), P("rows", None)),
        out_specs=(P(("rows", "cols"), None), P("cols", None)),
        check_vma=False,
    )
```

```python
import jax
import jax.numpy as jnp
from jax import lax
from jax.experimental import pallas as pl
from jax.experimental.pallas import tpu as pltpu
from jax.sharding import PartitionSpec as P

MESH = pl.DeviceIdType.MESH
BF, F32 = jnp.bfloat16, jnp.float32

TILE = 64
OWN = 16
GROUP = 256
WIN = 768
SCALE = 1.0 / 16384

A2A, TIL, IDX, VEC, EARLY, OLD, LATE = 0, 16, 22, 24, 26, 28, 30
QUART, GATH, PAIR, XRED, ZRED, SPREAD, RELAY, COUNT = 32, 36, 52, 56, 72, 80, 88, 96


def swap(v):
    return jnp.concatenate([v[:, 64:], v[:, :64]], axis=1)


def pack(block):
    return jnp.concatenate([block[:32], block[32:]], axis=1)


def kernel(
    x_hbm, cols_hbm, tiles_hbm, out_ref, gram_ref,
    x_ref, cols_ref, xs, xr, tv, th, idxv, idxh, idxs, slab, band, hx, hp, ho, w0, w1, y0, y1,
    fp, op, fq, pc, fy, gs, gr, gf, xsnd, xrcv, zs, zr, ro, local_sem, ss, rs,
):
    r, c = lax.axis_index("rows"), lax.axis_index("cols")
    yy, zh = lax.rem(c, 4), c // 4
    core, x, zl = lax.rem(r, 2), lax.rem(r // 2, 4), r // 8
    z = zh * 2 + zl
    w, y = (w0, w1), (y0, y1)

    def remote(src, dst, number, device):
        return pltpu.make_async_remote_copy(
            src_ref=src, dst_ref=dst, send_sem=ss.at[number], recv_sem=rs.at[number],
            device_id=device, device_id_type=MESH,
        )

    own_x = pltpu.make_async_copy(x_hbm, x_ref, local_sem.at[0])
    own_cols = pltpu.make_async_copy(cols_hbm, cols_ref, local_sem.at[1])
    own_tiles = pltpu.make_async_copy(tiles_hbm, tv, local_sem.at[2])

    barrier = pltpu.get_barrier_semaphore()

    def greet(device):
        pl.semaphore_signal(barrier, inc=1, device_id=device, device_id_type=MESH)

    for i in (8, 7, 9, 6, 10, 5, 11, 4, 12, 3, 13, 2, 14, 1, 15):
        greet((r, lax.rem(c + i, 16)))
    for i in range(4):
        greet((lax.rem(r + 8, 16), lax.rem(zh + i, 4) * 4 + yy))
    for i in range(1, 8):
        greet((zl * 8 + lax.rem(r + i, 8), c))
    at_7, at_8 = r == 7, r == 8
    middle = jnp.logical_or(at_7, at_8)
    turned = jnp.where(at_7, lax.rem(zh + 3, 4), lax.rem(zh + 1, 4)) * 4 + yy
    @pl.when(middle)
    def _():
        greet((15 - r, c))
        greet((15 - r, turned))

    own_x.start()
    own_cols.start()
    own_tiles.start()

    has_low, has_high = r > 0, r < 15
    edges = (has_low, has_high)
    up, down = jnp.minimum(r + 1, 15), jnp.maximum(r - 1, 0)

    def zero(ref, first, count):
        ref[pl.ds(first, count), :] = jnp.zeros((count, ref.shape[1]), ref.dtype)

    for side in range(2):

        @pl.when(jnp.logical_not(edges[side]))
        def _(side=side):
            zero(band, 7 * side * GROUP, 3 * GROUP)
            zero(w[0], side * 8 * GROUP, 4 * GROUP)

    for u in range(4):
        slab[u, 8] = jnp.zeros((TILE, 128), BF)

    own_x.wait()
    for g in range(16):
        xs[g] = pack(x_ref[:, g * 64 : (g + 1) * 64])

    own_cols.wait()
    slot = lax.broadcasted_iota(jnp.int32, (16, OWN), 0)
    first_col = r * OWN + (lax.broadcasted_iota(jnp.int32, (8, OWN), 1) // 4) * 4 - 4
    places = cols_ref[...] - first_col
    slabs = jnp.full((16, OWN), 8, jnp.int32)
    for k in range(8):
        which = jnp.where(lax.rem(slot, 2) == 0, k, k + 1 - 2 * (k % 2))
        slabs = jnp.where(slot == places[k : k + 1, :], which, slabs)
    idxv[...] = jnp.zeros_like(idxv)
    idxv[:, :OWN] = slabs

    pl.when(middle)(lambda: pl.semaphore_wait(barrier, 28))
    pl.when(jnp.logical_not(middle))(lambda: pl.semaphore_wait(barrier, 26))

    a2a = []
    for i in (8, 7, 9, 6, 10, 5, 11, 4, 12, 3, 13, 2, 14, 1, 15):
        to = lax.rem(c + i, 16)
        copy = remote(xs.at[to], xr.at[c], A2A + i, (r, to))
        copy.start()
        a2a.append(copy)

    def both_sides(number, to_up, to_down, low_dst, high_dst, col_up=c, col_down=c):
        a = remote(to_up, low_dst, number, (up, col_up))
        b = remote(to_down, high_dst, number + 1, (down, col_down))
        pl.when(has_high)(a.start)
        pl.when(has_low)(b.start)
        return a, b

    def arrived(pair):
        pl.when(has_low)(pair[0].wait_recv)
        pl.when(has_high)(pair[1].wait_recv)

    def sent(pair):
        pl.when(has_high)(pair[0].wait_send)
        pl.when(has_low)(pair[1].wait_send)

    idx = both_sides(IDX, idxv, idxv, idxh.at[0], idxh.at[1])
    def on_fast(fast, work):
        for side in range(2):
            here = core == (1 - side if fast else side)
            pl.when(jnp.logical_and(here, edges[side]))(lambda side=side: work(side))

    mine_of = [th.at[side, 2, pl.ds(yy, 1)] for side in range(2)]
    whole = (
        remote(tiles_hbm.at[pl.ds(4, 4)], th.at[0, 2], TIL + 4, (up, c)),
        remote(tiles_hbm.at[pl.ds(8, 4)], th.at[1, 2], TIL + 5, (down, c)),
    )
    shared = (
        remote(tiles_hbm.at[pl.ds(4 + yy, 1)], mine_of[0], TIL + 4, (up, c)),
        remote(tiles_hbm.at[pl.ds(8 + yy, 1)], mine_of[1], TIL + 5, (down, c)),
    )

    def far_out(method):
        pl.when(jnp.logical_and(core == 1, has_high))(lambda: getattr(shared[0], method)())
        pl.when(jnp.logical_and(core == 0, has_low))(lambda: getattr(shared[1], method)())
        pl.when(core == 0)(lambda: getattr(whole[0], method)())
        pl.when(core == 1)(lambda: getattr(whole[1], method)())

    far_out("start")
    til = [
        both_sides(
            TIL + 2 * n, tiles_hbm.at[pl.ds(4 * (3 - n), 4)], tiles_hbm.at[pl.ds(4 * n, 4)],
            th.at[0, n], th.at[1, n],
            *((jnp.where(at_7, turned, c), jnp.where(at_8, turned, c)) if n == 1 else (c, c)),
        )
        for n in range(2)
    ]
    relay = [
        [
            remote(v, v, RELAY + 4 * side + j, (r, zh * 4 + lax.rem(yy + j, 4)))
            for j in (2, 1, 3)
        ]
        for side, v in enumerate(mine_of)
    ]

    xr[c] = xs[c]

    low_lanes = lax.broadcasted_iota(jnp.int32, (TILE, 128), 1) < 64

    def place(tiles, source, first, at):
        for u in range(4):
            for p in range(4):
                piece = tiles[u, :, p * 128 : (p + 1) * 128]
                slab[u, 2 * p] = piece
                slab[u, 2 * p + 1] = swap(piece)
            for j in range(6):
                left = slab[u, idxs[source, 2 * j, first + u]]
                right = slab[u, idxs[source, 2 * j + 1, first + u]]
                band[pl.ds(at + u * TILE, TILE), j * 128 : (j + 1) * 128] = jnp.where(
                    low_lanes, left, right
                )

    def to_smem(src, number):
        copy = pltpu.make_async_copy(src, idxs.at[number], local_sem.at[3])
        copy.start()
        copy.wait()

    to_smem(idxv, 2)
    own_tiles.wait()

    def place_own(i, carry):
        at = pl.multiple_of((3 + i) * GROUP, GROUP)
        place(tv.at[pl.ds(4 * i, 4)], 2, 4 * i, at)
        return carry

    lax.fori_loop(0, 4, place_own, 0)

    def pass_on(side):
        shared[side].wait_recv()
        for copy in relay[side]:
            copy.start()

    on_fast(False, pass_on)

    arrived(idx)
    for side in range(2):

        @pl.when(edges[side])
        def _(side=side):
            to_smem(idxh.at[side], side)

    def unpack(v, block, ref):
        for half in range(2):
            rows = pl.ds(block * TILE + half * 32, 32)
            ref[rows, :] = v[:, half * 64 : (half + 1) * 64].astype(ref.dtype)

    def one(n, k, turn=False):
        g = jnp.where(core == 0, k, 11 - k) if turn else k
        now, later = n % 2, (n + 1) % 2
        at = g * GROUP if isinstance(g, int) else pl.multiple_of(g * GROUP, GROUP)
        back = (g - 1) * GROUP if isinstance(g, int) else pl.multiple_of((g - 1) * GROUP, GROUP)
        rows = pl.ds(at, GROUP)
        product = jnp.dot(
            band[pl.ds(back, GROUP), :], w[now][pl.ds(back, WIN), :], preferred_element_type=F32
        )
        outer = n in (4, 5) and not 4 <= k <= 7
        current = w[now][rows, :].astype(F32) if n == 0 or (n == 4 and outer) else y[now][rows, :]
        if n == 0:
            new = (product - 0.1 * current) * 0.5
        else:
            before = w if n == 1 or (n == 5 and outer) else y
            new = product - 0.1 * current - before[later][rows, :].astype(F32)
        rounded = new.astype(BF)
        if n < 7:
            y[later][rows, :] = new
            w[later][rows, :] = rounded
        return rounded

    for copy in a2a:
        copy.wait_recv()
    vec = both_sides(VEC, xr, xr, hx.at[0], hx.at[1])
    for b in range(OWN):
        unpack(xr[b], OWN + b, w[0])
    for g in (5, 6):
        one(0, g)

    def place_chunk(side, n):
        place(
            th.at[side, n], side, 4 * (3 - n) if side == 0 else 4 * n,
            (2 - n if side == 0 else 7 + n) * GROUP,
        )

    def near_chunks(side):
        for n in range(2):
            til[n][side].wait_recv()
            place_chunk(side, n)

    def vectors(side):
        vec[side].wait_recv()
        for b in range(OWN):
            unpack(hx[side, b], side * 2 * OWN + b, w[0])

    def far_chunk_here(side):
        whole[side].wait_recv()
        place_chunk(side, 2)

    def far_chunk(side):
        for copy in relay[side]:
            copy.wait_recv()
        place_chunk(side, 2)

    on_fast(True, near_chunks)
    on_fast(True, far_chunk_here)
    on_fast(True, vectors)
    for n, k in ((0, 7), (0, 8), (0, 9), (1, 6), (1, 7), (1, 8), (2, 7)):
        one(n, k, True)
    on_fast(False, near_chunks)
    on_fast(False, vectors)
    for n, k in ((0, 4), (0, 3), (0, 2), (1, 5), (1, 4), (1, 3), (2, 6), (2, 5), (2, 4)):
        one(n, k, True)

    for b in range(8):
        op[b] = pack(y[1][pl.ds((20 + b) * TILE, TILE), :]).astype(BF)
    old = both_sides(OLD, op, op, ho.at[0], ho.at[1])

    def pack_group(rounded, dst, first):
        for b in range(4):
            dst[first + b] = pack(rounded[b * TILE : (b + 1) * TILE])

    for slot, g in ((0, 5), (4, 6)):
        pack_group(one(3, g), fp, slot)
    early = both_sides(
        EARLY, fp.at[pl.ds(0, 8)], fp.at[pl.ds(0, 8)], hp.at[0, pl.ds(0, 8)], hp.at[1, pl.ds(0, 8)]
    )
    on_fast(False, far_chunk)
    for n, g in ((0, 1), (0, 10), (1, 2), (1, 9), (2, 3), (2, 8)):
        one(n, g)
    for slot, g in ((8, 4), (12, 7)):
        pack_group(one(3, g), fp, slot)
    late = both_sides(
        LATE, fp.at[pl.ds(8, 8)], fp.at[pl.ds(8, 8)], hp.at[0, pl.ds(8, 8)], hp.at[1, pl.ds(8, 8)]
    )
    for g in (5, 6):
        one(4, g)

    def later_vectors(side):
        for pair in (old, early, late):
            pair[side].wait_recv()
        first = side * 2 * OWN
        for b in range(8):
            unpack(hp[side, b], first + 4 + b, w[0])
            unpack(ho[side, b], first + 4 + b, y[1])
            unpack(hp[side, 8 + b], first + (b if b < 4 else b + 8), w[0])

    on_fast(True, later_vectors)
    for n, ks in ((4, (7, 8, 9, 10)), (5, (6, 7, 8, 9)), (6, (7, 8))):
        for k in ks:
            one(n, k, True)
    on_fast(False, later_vectors)
    for n, ks in ((4, (4, 3, 2, 1)), (5, (5, 4, 3, 2)), (6, (6, 5, 4, 3))):
        for k in ks:
            one(n, k, True)

    quart, gath = [], {}
    for i in (2, 1, 3, 0):
        to = lax.rem(zh + i, 4)
        rounded = one(7, 4 + to)
        if i:
            pack_group(rounded, fq.at[to], 0)
            copy = remote(fq.at[to], pc.at[yy, zh], QUART + i, (r, to * 4 + yy))
            copy.start()
            quart.append((i, copy))
        else:
            pack_group(rounded, pc.at[yy, zh], 0)

    def to_y(i):
        piece = pc.at[yy, lax.rem(zh - i + 4, 4)]
        for j in (2, 1, 3):
            device = (r, zh * 4 + lax.rem(yy + j, 4))
            copy = remote(piece, piece, GATH + 4 * i + j, device)
            copy.start()
            gath[i, j] = copy

    to_y(0)
    for i, copy in (quart[1], quart[2], quart[0]):
        copy.wait_recv()
        to_y(i)

    def assemble(who):
        for half in range(2):
            for b in range(4):
                left, right = pc[who, 2 * half, b], pc[who, 2 * half + 1, b]
                for part in range(2):
                    lanes = slice(part * 64, (part + 1) * 64)
                    fy[2 * who + half, pl.ds(b * TILE + part * 32, 32), :] = jnp.concatenate(
                        [left[:, lanes], right[:, lanes]], axis=1
                    )

    assemble(yy)
    mine = jnp.concatenate(
        [fy[2 * yy + half].astype(F32).T.astype(BF) for half in range(2)], axis=0
    )
    for j in (1, 3, 2):
        for i in range(4):
            gath[i, j].wait_recv()
        assemble(lax.rem(yy - j + 4, 4))

    pair_dev = (r + 1 - 2 * core, c)
    order = (2, 1, 3, 0)
    pairs = {}
    for i in order:
        to = lax.rem(x + i, 4)
        gs[i] = jnp.dot(mine, fy[(1 - core) * 4 + to], preferred_element_type=F32).astype(BF)
        pairs[i] = remote(gs.at[i], gr.at[i], PAIR + i, pair_dev)
        pairs[i].start()
    for i in order:
        gf[i] = jnp.dot(mine, fy[core * 4 + lax.rem(x + i, 4)], preferred_element_type=F32)

    xred = {}
    parts = [lax.rem(zh + d, 4) for d in (2, 1, 3, 0)]
    for i in order:
        pairs[i].wait_recv()
        total = gf[i] + gr[i].astype(F32)
        if i:
            xsnd[i] = total.astype(BF)
        else:
            gf[0] = total
    for k, part in enumerate(parts):
        rows = pl.ds(pl.multiple_of(part * 64, 64), 64)
        for i in order[:3]:
            device = (zl * 8 + lax.rem(x + i, 4) * 2 + core, c)
            xred[i, k] = remote(xsnd.at[i, rows], xrcv.at[i, rows], XRED + 4 * i + k, device)
            xred[i, k].start()

    rows = pl.ds(pl.multiple_of(yy * TILE, TILE), TILE)
    for h in range(4):
        for p in range(2):
            lanes = slice((h % 2) * 64, (h % 2 + 1) * 64)
            out_ref[:, h * 256 + p * 128 : h * 256 + (p + 1) * 128] = jnp.concatenate(
                [fy[4 * p + h // 2, rows, lanes], fy[4 * p + 2 + h // 2, rows, lanes]], axis=1
            )

    for k, part in enumerate(parts):
        rows = pl.ds(pl.multiple_of(part * 64, 64), 64)
        total = gf[0, rows, :]
        for i in order[:3]:
            xred[i, k].wait_recv()
            total = total + xrcv[i, rows, :].astype(F32)
        zs[rows, :] = total.astype(BF)
        for lo in (zl, 1 - zl) if k < 3 else (1 - zl,):
            i = lax.rem(part * 2 + lo - z + 8, 8)
            copy = remote(zs.at[rows], zr.at[z], ZRED + i, (lo * 8 + x * 2 + core, part * 4 + yy))
            copy.start()
    zr[z] = zs[pl.ds(pl.multiple_of(zh * 64, 64), 64), :]
    landed = [remote(zs.at[pl.ds(0, 64)], zr.at[z], ZRED + i, pair_dev) for i in range(1, 8)]
    for copy in landed:
        copy.wait_recv()
    total = zr[0].astype(F32)
    for i in range(1, 8):
        total = total + zr[i].astype(F32)
    rr = lax.rem(r, 8)
    ro[rr] = (total * SCALE).astype(BF)

    spread = []
    for i in (4, 3, 5, 2, 6, 7, 1):
        copy = remote(ro.at[rr], ro.at[rr], SPREAD + i, (zl * 8 + lax.rem(rr + i, 8), c))
        copy.start()
        spread.append(copy)

    def passed_on(side):
        for copy in relay[side]:
            copy.wait_send()

    on_fast(False, passed_on)
    far_out("wait_send")
    for pair in (idx, *til, vec, old, early, late):
        sent(pair)
    for copy in a2a + list(gath.values()):
        copy.wait_send()
    for i, copy in quart + list(pairs.items()):
        copy.wait_send()
    for copy in list(xred.values()) + landed:
        copy.wait_send()
    for copy in spread:
        copy.wait_recv()
    for h in range(4):
        for p in range(2):
            lanes = slice((h % 2) * 64, (h % 2 + 1) * 64)
            at = [(k * 2 + h // 2) * 2 + p for k in range(2)]
            gram_ref[:, h * 256 + p * 128 : h * 256 + (p + 1) * 128] = jnp.concatenate(
                [ro[at[0]][:, lanes], ro[at[1]][:, lanes]], axis=1
            ).astype(F32)
    for copy in spread:
        copy.wait_send()


def per_device(search_vectors, tile_values, block_columns):
    ext = 12 * GROUP
    return pl.pallas_call(
        kernel,
        out_shape=(
            jax.ShapeDtypeStruct((64, 1024), BF),
            jax.ShapeDtypeStruct((64, 1024), F32),
        ),
        in_specs=[pl.BlockSpec(memory_space=pl.ANY)] * 3,
        out_specs=(pl.BlockSpec(memory_space=pltpu.VMEM), pl.BlockSpec(memory_space=pltpu.VMEM)),
        scratch_shapes=[
            pltpu.VMEM((64, 1024), BF),
            pltpu.VMEM((8, OWN), jnp.int32),
            pltpu.VMEM((16, 32, 128), BF),
            pltpu.VMEM((16, 32, 128), BF),
            pltpu.VMEM((OWN, TILE, 512), BF),
            pltpu.VMEM((2, 3, 4, TILE, 512), BF),
            pltpu.VMEM((16, 128), jnp.int32),
            pltpu.VMEM((2, 16, 128), jnp.int32),
            pltpu.SMEM((3, 16, 128), jnp.int32),
            pltpu.VMEM((4, 9, TILE, 128), BF),
            pltpu.VMEM((10 * GROUP, WIN), BF),
            pltpu.VMEM((2, 16, 32, 128), BF),
            pltpu.VMEM((2, 16, 32, 128), BF),
            pltpu.VMEM((2, 8, 32, 128), BF),
            pltpu.VMEM((ext, 64), BF),
            pltpu.VMEM((ext, 64), BF),
            pltpu.VMEM((ext, 64), F32),
            pltpu.VMEM((ext, 64), F32),
            pltpu.VMEM((16, 32, 128), BF),
            pltpu.VMEM((8, 32, 128), BF),
            pltpu.VMEM((4, 4, 32, 128), BF),
            pltpu.VMEM((4, 4, 4, 32, 128), BF),
            pltpu.VMEM((8, 256, 128), BF),
            pltpu.VMEM((4, 256, 128), BF),
            pltpu.VMEM((4, 256, 128), BF),
            pltpu.VMEM((4, 256, 128), F32),
            pltpu.VMEM((4, 256, 128), BF),
            pltpu.VMEM((4, 256, 128), BF),
            pltpu.VMEM((256, 128), BF),
            pltpu.VMEM((8, 64, 128), BF),
            pltpu.VMEM((8, 64, 128), BF),
            pltpu.SemaphoreType.DMA((4,)),
            pltpu.SemaphoreType.DMA((COUNT,)),
            pltpu.SemaphoreType.DMA((COUNT,)),
        ],
        compiler_params=pltpu.CompilerParams(
            collective_id=0, has_side_effects=True, vmem_limit_bytes=48 * 1024 * 1024
        ),
        name="filter_and_gram",
    )(*(pltpu.with_memory_space_constraint(v, pltpu.HBM) for v in (search_vectors, block_columns.T, tile_values)))


def solution(mesh):
    return jax.shard_map(
        per_device,
        mesh=mesh,
        in_specs=(P(("rows", "cols"), None), P("rows", None, None), P("rows", None)),
        out_specs=(P(("rows", "cols"), None), P("cols", None)),
        check_vma=False,
    )
```
